32 devices in a mesh: sensor: 16 (over z, y, core), day: 2 (over x).
Axes of the slice: x: 2, y: 2, z: 4, core: 2. Of those that a mesh axis runs over, the one named last changes fastest.
Arguments:
- y_obs: bfloat16 [2880, 2048], P('day', 'sensor'), may hold values from -256 to 256
- observed: int32 [2880, 2048], P('day', 'sensor'), may hold values 0 or 1
- day_factor: bfloat16 [10, 64], P('day'), may hold values from -6 to 6
- slot_factor: bfloat16 [288, 64], P('day'), may hold values from -6 to 6
- sensor_factor: bfloat16 [64, 2048], P(None, 'sensor'), may hold values from -6 to 6
- prior_scale: float32 [64], replicated, may hold values from 0.5 to 2
- neighbours: int32 [6, 2048], P(None, 'sensor'), may hold values from 0 to 2047, as said below
- edge_weight: float32 [6, 2048], P(None, 'sensor'), may hold values from 0.2 to 1
- noise: float32 [64, 2048], P(None, 'sensor'), may hold values from -6 to 6
Outputs:
- fresh_factor: float32 [64, 2048], P(None, 'sensor')
The draws below stay inside these ranges and needn't reach their ends.
Inputs may be any that keep to these rules, and one draw needn't show every extreme that they name: Each sensor's neighbours are other sensors within 256 of it in index; its first two lie exactly that far away.
All inputs are finite; a program needn't handle non-finite values. No bound on the sum of `observed` on one device may be relied on, other than what follows from the above.
Results may differ from the reference program's by a relative error of at most 0.0023.
Values may be sent and summed in bfloat16 or wider, within the bound.
A program may use at most 64 MiB of HBM per device.

```python
import math
import jax
import jax.numpy as jnp
from jax import lax

R = 64
SLOTS = 288
NB = 6
SENS_DEV = 128
SENSORS = 2048
DAYS = 10
ROWS = 2880


def draw_neighbours(key, part):
    span = 2 * SENS_DEV
    sensor_ids = jnp.arange(SENSORS, dtype=jnp.int32)[None, :]
    key_size, key_sign = jax.random.split(key)
    magnitude = jax.random.randint(key_size, (NB, SENSORS), 1, span + 1)
    signs = 2 * jax.random.randint(key_sign, (NB, SENSORS), 0, 2) - 1
    offsets = magnitude * signs
    first_row = jnp.full((1, SENSORS), span, dtype=jnp.int32)
    second_row = jnp.where(sensor_ids >= span, -span, span).astype(jnp.int32)
    offsets = jnp.concatenate([first_row, second_row, offsets[2:]], axis=0)
    candidate = sensor_ids + offsets
    outside = (candidate < 0) | (candidate >= SENSORS)
    return jnp.where(outside, sensor_ids - offsets, candidate).astype(jnp.int32)


def plant(result, stream_key, low, largest):
    shape = result.shape
    index_at = [jax.random.randint(jax.random.fold_in(stream_key, axis), (), 0, shape[axis]) for axis in range(len(shape))]
    result = result.at[tuple(index_at)].set(low)
    longest = shape.index(max(shape))
    index_at[longest] = (index_at[longest] + 1) % shape[longest]
    return result.at[tuple(index_at)].set(largest)


def level_of(own_key, shape, pieces, smallest, top_value):
    def one(dim, blocks):
        steps = jax.random.uniform(jax.random.fold_in(jax.random.fold_in(own_key, 6), dim), (blocks,), jnp.float32, smallest / len(pieces), top_value / len(pieces))
        return jnp.repeat(jnp.exp(steps), shape[dim] // blocks).reshape((-1,) + (1,) * (len(shape) - dim - 1))

    factor_of = one(*pieces[0])
    for cut in pieces[1:]:
        factor_of = factor_of * one(*cut)
    return factor_of


def scatter_about(stream_key, shape, deviation, limit, cuts=(), held_as=jnp.bfloat16):
    array = jax.random.normal(stream_key, shape, jnp.float32) * deviation
    if len(cuts) > 0:
        array = level_of(stream_key, shape, cuts, -0.22, 0.18) * array
    return jnp.clip(array, min=-limit, max=limit).astype(held_as)


def setup_inputs(seed: int = 0) -> dict:
    seeds = jax.random.split(jax.random.key(seed), 10)
    y_obs = scatter_about(seeds[0], (ROWS, SENSORS), 40.0, 256.0, ((0, 2), (1, 16)))
    observed = plant((jax.random.randint(seeds[1], (ROWS, SENSORS), 0, 2) < 1).astype(jnp.int32), jax.random.fold_in(seeds[1], 1), 0, 1)
    day_factor = scatter_about(seeds[2], (DAYS, R), 1.0, 6.0, ((0, 2),))
    slot_factor = scatter_about(seeds[3], (SLOTS, R), 1.0, 6.0, ((0, 2),))
    sensor_factor = scatter_about(seeds[4], (R, SENSORS), 1.0, 6.0, ((1, 16),))
    prior_scale = jnp.clip(jnp.exp(jax.random.uniform(seeds[5], (R,), jnp.float32, math.log(0.5), math.log(2.0))), 0.5, 2.0)
    neighbours = draw_neighbours(jax.random.fold_in(seeds[9], 71), 0)
    edge_weight = jnp.clip(jnp.exp(math.log(1.0) - 1.609438 * jax.random.uniform(seeds[7], (NB, SENSORS), jnp.float32) ** level_of(seeds[7], (NB, SENSORS), ((1, 16),), -0.2, 0.2)), 0.2, 1.0)
    noise = scatter_about(seeds[8], (R, SENSORS), 0.5, 6.0, ((1, 16),), jnp.float32)
    return dict(y_obs=y_obs, observed=observed, day_factor=day_factor, slot_factor=slot_factor, sensor_factor=sensor_factor, prior_scale=prior_scale, neighbours=neighbours, edge_weight=edge_weight, noise=noise)


def solve_block(gram_sums, right_sums, pulled, prior_diag, prior_scale, noise_rows, tau):
    count = gram_sums.shape[0]
    rank = right_sums.shape[1]
    squares = gram_sums.reshape(count, rank, rank)
    precision = tau * squares + prior_diag[:, None, None] * jnp.diag(prior_scale)[None, :, :]
    target = tau * right_sums + prior_scale[None, :] * pulled
    factor_low = jnp.linalg.cholesky(precision)
    halfway = lax.linalg.triangular_solve(factor_low, target[:, :, None], left_side=True, lower=True)
    centre_part = lax.linalg.triangular_solve(factor_low, halfway, left_side=True, lower=True, transpose_a=True)
    spread_part = lax.linalg.triangular_solve(factor_low, noise_rows[:, :, None], left_side=True, lower=True, transpose_a=True)
    return (centre_part + spread_part)[:, :, 0]

def reference(y_obs, observed, day_factor, slot_factor, sensor_factor, prior_scale, neighbours, edge_weight, noise):
    features = (day_factor.astype(jnp.float32)[:, None, :] * slot_factor.astype(jnp.float32)[None, :, :]).reshape(ROWS, R).astype(jnp.bfloat16)
    wide = features.astype(jnp.float32)
    outer_rows = (wide[:, :, None] * wide[:, None, :]).reshape(ROWS, R * R).astype(jnp.bfloat16)
    mask_float = observed.astype(jnp.float32)
    weighted = (mask_float * y_obs.astype(jnp.float32)).astype(jnp.bfloat16)
    dims = (((0,), (0,)), ((), ()))
    gram_sums = lax.dot_general(mask_float, outer_rows.astype(jnp.float32), dims, precision=lax.Precision.HIGHEST)
    right_sums = lax.dot_general(weighted.astype(jnp.float32), wide, dims, precision=lax.Precision.HIGHEST)
    picked = jnp.take(sensor_factor, neighbours, axis=1).astype(jnp.float32)
    pulled = jnp.einsum('rns,ns->sr', picked, edge_weight)
    prior_diag = 1.0 + jnp.sum(edge_weight, axis=0)
    tau = 4.0 / ROWS
    solved = solve_block(gram_sums, right_sums, pulled, prior_diag, prior_scale, noise.T, tau)
    return solved.T
```

```python
import jax
import jax.numpy as jnp
from jax import lax
from jax.experimental import pallas as pl
from jax.experimental.pallas import tpu as pltpu
from jax.sharding import PartitionSpec as P

RANK = 64
LANES = 128
HALF = 64
BLOCKS = RANK // 8


def lane_low(shape):
    return lax.broadcasted_iota(jnp.int32, shape, len(shape) - 1) < HALF


def both_halves(tile, upper):
    other = pltpu.roll(tile, HALF, 1)
    low = lane_low(tile.shape)
    return jnp.where(low, other, tile) if upper else jnp.where(low, tile, other)


def row_of(tile, index):
    return jnp.broadcast_to(tile[index : index + 1, :], tile.shape)


def factor_and_solve(load_columns, target, noise_tile, cols, wide, inv_diag, halfway, found):
    target = list(target)
    for block in range(BLOCKS):
        first = block // 2
        upper = block % 2 == 1
        count = 4 - first
        columns = load_columns(block)
        if block > 0:

            def subtract(k, carry):
                done = [cols[k, pl.ds(8 * q, 8), :] for q in range(first, 4)]
                out = []
                for c in range(8):
                    scale = jnp.broadcast_to(wide[k, pl.ds(8 * block + c, 1), :], (8, LANES))
                    out.extend(carry[c * count + q] - done[q] * scale for q in range(count))
                return tuple(out)

            flat = tuple(tile for column in columns for tile in column)
            flat = lax.fori_loop(0, 8 * block, subtract, flat, unroll=2)
            columns = [list(flat[c * count : (c + 1) * count]) for c in range(8)]
        corner = [both_halves(column[0], upper) for column in columns]
        side = both_halves(target[first], upper)
        for c in range(8):
            j = 8 * block + c
            inverse = lax.rsqrt(row_of(corner[c], c))
            corner[c] = corner[c] * inverse
            columns[c] = [tile * inverse for tile in columns[c]]
            solved = row_of(side, c) * inverse
            side = side - corner[c] * solved
            for q in range(count):
                target[first + q] = target[first + q] - columns[c][q] * solved
            for later in range(c + 1, 8):
                scale = row_of(corner[c], later)
                corner[later] = corner[later] - corner[c] * scale
                columns[later] = [
                    tile - own * scale for tile, own in zip(columns[later], columns[c])
                ]
            inv_diag[j] = inverse
            halfway[pl.ds(j, 1), :] = solved[0:1, :]
        for c in range(8):
            j = 8 * block + c
            for q in range(count):
                tile = columns[c][q]
                row = 16 * (first + q)
                cols[j, pl.ds(8 * (first + q), 8), :] = tile
                if row >= 8 * block:
                    wide[j, pl.ds(row, 8), :] = both_halves(tile, False)
                wide[j, pl.ds(row + 8, 8), :] = both_halves(tile, True)

    packed = [None] * 4
    low = lane_low((8, LANES))
    below = None
    for block in reversed(range(BLOCKS)):
        first = block // 2
        upper = block % 2 == 1
        right = halfway[pl.ds(8 * block, 8), :] + noise_tile(block)
        remain = []
        for c in range(8):
            j = 8 * block + c
            total = row_of(right, c)
            parts = None
            for q in range(first, 4):
                if q == first and upper:
                    continue
                if q == first:
                    term = jnp.where(low, 0.0, cols[j, pl.ds(8 * q, 8), :] * below)
                else:
                    term = cols[j, pl.ds(8 * q, 8), :] * packed[q]
                parts = term if parts is None else parts + term
            if parts is not None:
                sums = jnp.sum(parts, axis=0, keepdims=True)
                sums = jnp.broadcast_to(sums, (8, LANES))
                total = total - (sums + pltpu.roll(sums, HALF, 1))
            remain.append(total)
        values = [None] * 8
        for c in reversed(range(8)):
            values[c] = remain[c] * inv_diag[8 * block + c]
            for earlier in range(c):
                scale = jnp.broadcast_to(
                    wide[8 * block + earlier, pl.ds(8 * block + c, 1), :], (8, LANES)
                )
                remain[earlier] = remain[earlier] - scale * values[c]
        rows = lax.broadcasted_iota(jnp.int32, (8, LANES), 0)
        tile = values[0]
        for c in range(1, 8):
            tile = jnp.where(rows == c, values[c], tile)
        found[pl.ds(8 * block, 8), :] = tile
        if upper:
            below = tile
        else:
            packed[first] = jnp.where(low, tile, below)
            below = None
    return packed


def diagonal_tile(block, c, value):
    shape = (8, LANES)
    rows = lax.broadcasted_iota(jnp.int32, shape, 0)
    low = lane_low(shape)
    half = low if block % 2 == 0 else jnp.logical_not(low)
    return jnp.where((rows == c) & half, value, 0.0)


def solve_kernel(squares, target, noise, prior, out, cols, wide, inv_diag, halfway):
    def load_columns(block):
        first = block // 2
        own = prior[pl.ds(8 * block, 8), :]
        columns = []
        for c in range(8):
            j = 8 * block + c
            tiles = [squares[j, pl.ds(8 * q, 8), :] for q in range(first, 4)]
            tiles[0] = tiles[0] + diagonal_tile(block, c, own)
            columns.append(tiles)
        return columns

    targets = [target[pl.ds(8 * q, 8), :] for q in range(4)]
    factor_and_solve(
        load_columns,
        targets,
        lambda block: noise[pl.ds(8 * block, 8), :],
        cols,
        wide,
        inv_diag,
        halfway,
        out,
    )


def solver_scratch():
    return [
        pltpu.VMEM((RANK, 32, LANES), jnp.float32),
        pltpu.VMEM((RANK, RANK, LANES), jnp.float32),
        pltpu.VMEM((RANK, 8, LANES), jnp.float32),
        pltpu.VMEM((RANK, LANES), jnp.float32),
    ]


def pack_rows(rows):
    lead = rows.shape[:-2]
    split = rows.reshape(lead + (4, 2, 8, HALF))
    return jnp.swapaxes(split, -3, -2).reshape(lead + (32, LANES))


def solve_block(gram, right, pulled, prior_diag, prior_scale, noise, tau):
    share = right.shape[1]

    def fill(array, value=0.0):
        pad = [(0, 0)] * (array.ndim - 1) + [(0, HALF - share)]
        return jnp.pad(array, pad, constant_values=value)

    target = tau * right + prior_scale[:, None] * pulled
    prior = prior_scale[:, None] * fill(prior_diag, 1.0)[None, :]
    twice = lambda array: jnp.concatenate([array, array], axis=1)
    spec = pl.BlockSpec(memory_space=pltpu.VMEM)
    solved = pl.pallas_call(
        solve_kernel,
        out_shape=jax.ShapeDtypeStruct((RANK, LANES), jnp.float32),
        in_specs=[spec] * 4,
        out_specs=spec,
        scratch_shapes=solver_scratch(),
        compiler_params=pltpu.CompilerParams(vmem_limit_bytes=24 * 1024 * 1024),
        name="solve_sensors",
    )(tau * pack_rows(fill(gram)), pack_rows(fill(target)), twice(fill(noise)), twice(prior))
    return solved[:, :share]


def shifted(shard, axis, by):
    size = lax.axis_size(axis)
    pairs = [(i, i + by) for i in range(size) if 0 <= i + by < size]
    return lax.ppermute(shard, axis, pairs)


def general_shards(
    y_obs,
    observed,
    day_factor,
    slot_factor,
    sensor_factor,
    prior_scale,
    neighbours,
    edge_weight,
    noise,
):
    rank = sensor_factor.shape[0]
    block_len = sensor_factor.shape[1]
    all_slots = lax.all_gather(slot_factor, "day", axis=0, tiled=True)
    features = (day_factor[:, None, :] * all_slots[None, :, :]).reshape(-1, rank)
    row_total = features.shape[0] * lax.axis_size("day")
    outer_rows = (features[:, :, None] * features[:, None, :]).reshape(-1, rank * rank)
    mask_half = observed.astype(jnp.bfloat16)
    weighted = mask_half * y_obs
    dims = (((0,), (0,)), ((), ()))
    gram_sums = lax.dot_general(outer_rows, mask_half, dims, preferred_element_type=jnp.float32)
    right_sums = lax.dot_general(features, weighted, dims, preferred_element_type=jnp.float32)
    pieces = []
    for offset in (2, 1, 0, -1, -2):
        if offset == 0:
            pieces.append(sensor_factor)
        else:
            pieces.append(shifted(sensor_factor, "sensor", offset))
    window = jnp.concatenate(pieces, axis=1)
    base_col = (lax.axis_index("sensor") - 2) * block_len
    columns = neighbours - base_col
    picked = jnp.take(window, columns, axis=1).astype(jnp.float32)
    pulled = jnp.einsum("rns,ns->rs", picked, edge_weight)
    prior_diag = 1.0 + jnp.sum(edge_weight, axis=0)
    tau = 4.0 / row_total
    sums = jnp.concatenate([gram_sums, right_sums], axis=0)
    sums = lax.psum_scatter(sums, "day", scatter_dimension=1, tiled=True)
    share_len = sums.shape[1]
    first_col = lax.axis_index("day") * share_len
    part = lambda array: lax.dynamic_slice_in_dim(array, first_col, share_len, array.ndim - 1)
    solved = solve_block(
        sums[: rank * rank].reshape(rank, rank, share_len),
        sums[rank * rank :],
        part(pulled),
        part(prior_diag),
        prior_scale,
        part(noise),
        tau,
    )
    return lax.all_gather(solved, "day", axis=1, tiled=True)


def solution(mesh):
    return jax.shard_map(
        general_shards,
        mesh=mesh,
        in_specs=(
            P("day", "sensor"),
            P("day", "sensor"),
            P("day", None),
            P("day", None),
            P(None, "sensor"),
            P(),
            P(None, "sensor"),
            P(None, "sensor"),
            P(None, "sensor"),
        ),
        out_specs=P(None, "sensor"),
        check_vma=False,
    )
```

```python
import functools

import jax
import jax.numpy as jnp
from jax import lax
from jax.experimental import pallas as pl
from jax.experimental.pallas import tpu as pltpu
from jax.sharding import PartitionSpec as P

RANK = 64
LANES = 128
HALF = 64
BLOCKS = RANK // 8


def lane_low(shape):
    return lax.broadcasted_iota(jnp.int32, shape, len(shape) - 1) < HALF


def both_halves(tile, upper):
    other = pltpu.roll(tile, HALF, 1)
    low = lane_low(tile.shape)
    return jnp.where(low, other, tile) if upper else jnp.where(low, tile, other)


def row_of(tile, index):
    return jnp.broadcast_to(tile[index : index + 1, :], tile.shape)


def factor_and_solve(load_columns, target, noise_tile, cols, wide, inv_diag, halfway, found):
    target = list(target)
    for block in range(BLOCKS):
        first = block // 2
        upper = block % 2 == 1
        count = 4 - first
        columns = load_columns(block)
        if block > 0:

            def subtract(k, carry):
                done = [cols[k, pl.ds(8 * q, 8), :] for q in range(first, 4)]
                out = []
                for c in range(8):
                    scale = jnp.broadcast_to(wide[k, pl.ds(8 * block + c, 1), :], (8, LANES))
                    out.extend(carry[c * count + q] - done[q] * scale for q in range(count))
                return tuple(out)

            flat = tuple(tile for column in columns for tile in column)
            flat = lax.fori_loop(0, 8 * block, subtract, flat, unroll=2)
            columns = [list(flat[c * count : (c + 1) * count]) for c in range(8)]
        corner = [both_halves(column[0], upper) for column in columns]
        side = both_halves(target[first], upper)
        for c in range(8):
            j = 8 * block + c
            inverse = lax.rsqrt(row_of(corner[c], c))
            corner[c] = corner[c] * inverse
            columns[c] = [tile * inverse for tile in columns[c]]
            solved = row_of(side, c) * inverse
            side = side - corner[c] * solved
            for q in range(count):
                target[first + q] = target[first + q] - columns[c][q] * solved
            for later in range(c + 1, 8):
                scale = row_of(corner[c], later)
                corner[later] = corner[later] - corner[c] * scale
                columns[later] = [
                    tile - own * scale for tile, own in zip(columns[later], columns[c])
                ]
            inv_diag[j] = inverse
            halfway[pl.ds(j, 1), :] = solved[0:1, :]
        for c in range(8):
            j = 8 * block + c
            for q in range(count):
                tile = columns[c][q]
                row = 16 * (first + q)
                cols[j, pl.ds(8 * (first + q), 8), :] = tile
                if row >= 8 * block:
                    wide[j, pl.ds(row, 8), :] = both_halves(tile, False)
                wide[j, pl.ds(row + 8, 8), :] = both_halves(tile, True)

    packed = [None] * 4
    low = lane_low((8, LANES))
    below = None
    for block in reversed(range(BLOCKS)):
        first = block // 2
        upper = block % 2 == 1
        right = halfway[pl.ds(8 * block, 8), :] + noise_tile(block)
        remain = []
        for c in range(8):
            j = 8 * block + c
            total = row_of(right, c)
            parts = None
            for q in range(first, 4):
                if q == first and upper:
                    continue
                if q == first:
                    term = jnp.where(low, 0.0, cols[j, pl.ds(8 * q, 8), :] * below)
                else:
                    term = cols[j, pl.ds(8 * q, 8), :] * packed[q]
                parts = term if parts is None else parts + term
            if parts is not None:
                sums = jnp.sum(parts, axis=0, keepdims=True)
                sums = jnp.broadcast_to(sums, (8, LANES))
                total = total - (sums + pltpu.roll(sums, HALF, 1))
            remain.append(total)
        values = [None] * 8
        for c in reversed(range(8)):
            values[c] = remain[c] * inv_diag[8 * block + c]
            for earlier in range(c):
                scale = jnp.broadcast_to(
                    wide[8 * block + earlier, pl.ds(8 * block + c, 1), :], (8, LANES)
                )
                remain[earlier] = remain[earlier] - scale * values[c]
        rows = lax.broadcasted_iota(jnp.int32, (8, LANES), 0)
        tile = values[0]
        for c in range(1, 8):
            tile = jnp.where(rows == c, values[c], tile)
        found[pl.ds(8 * block, 8), :] = tile
        if upper:
            below = tile
        else:
            packed[first] = jnp.where(low, tile, below)
            below = None
    return packed


def diagonal_tile(block, c, value):
    shape = (8, LANES)
    rows = lax.broadcasted_iota(jnp.int32, shape, 0)
    low = lane_low(shape)
    half = low if block % 2 == 0 else jnp.logical_not(low)
    return jnp.where((rows == c) & half, value, 0.0)


def solve_kernel(squares, target, noise, prior, out, cols, wide, inv_diag, halfway):
    def load_columns(block):
        first = block // 2
        own = prior[pl.ds(8 * block, 8), :]
        columns = []
        for c in range(8):
            j = 8 * block + c
            tiles = [squares[j, pl.ds(8 * q, 8), :] for q in range(first, 4)]
            tiles[0] = tiles[0] + diagonal_tile(block, c, own)
            columns.append(tiles)
        return columns

    targets = [target[pl.ds(8 * q, 8), :] for q in range(4)]
    factor_and_solve(
        load_columns,
        targets,
        lambda block: noise[pl.ds(8 * block, 8), :],
        cols,
        wide,
        inv_diag,
        halfway,
        out,
    )


def solver_scratch():
    return [
        pltpu.VMEM((RANK, 32, LANES), jnp.float32),
        pltpu.VMEM((RANK, RANK, LANES), jnp.float32),
        pltpu.VMEM((RANK, 8, LANES), jnp.float32),
        pltpu.VMEM((RANK, LANES), jnp.float32),
    ]


def pack_rows(rows):
    lead = rows.shape[:-2]
    split = rows.reshape(lead + (4, 2, 8, HALF))
    return jnp.swapaxes(split, -3, -2).reshape(lead + (32, LANES))


def solve_block(gram, right, pulled, prior_diag, prior_scale, noise, tau):
    share = right.shape[1]

    def fill(array, value=0.0):
        pad = [(0, 0)] * (array.ndim - 1) + [(0, HALF - share)]
        return jnp.pad(array, pad, constant_values=value)

    target = tau * right + prior_scale[:, None] * pulled
    prior = prior_scale[:, None] * fill(prior_diag, 1.0)[None, :]
    twice = lambda array: jnp.concatenate([array, array], axis=1)
    spec = pl.BlockSpec(memory_space=pltpu.VMEM)
    solved = pl.pallas_call(
        solve_kernel,
        out_shape=jax.ShapeDtypeStruct((RANK, LANES), jnp.float32),
        in_specs=[spec] * 4,
        out_specs=spec,
        scratch_shapes=solver_scratch(),
        compiler_params=pltpu.CompilerParams(vmem_limit_bytes=24 * 1024 * 1024),
        name="solve_sensors",
    )(tau * pack_rows(fill(gram)), pack_rows(fill(target)), twice(fill(noise)), twice(prior))
    return solved[:, :share]


def shifted(shard, axis, by):
    size = lax.axis_size(axis)
    pairs = [(i, i + by) for i in range(size) if 0 <= i + by < size]
    return lax.ppermute(shard, axis, pairs)


def general_shards(
    y_obs,
    observed,
    day_factor,
    slot_factor,
    sensor_factor,
    prior_scale,
    neighbours,
    edge_weight,
    noise,
):
    rank = sensor_factor.shape[0]
    block_len = sensor_factor.shape[1]
    all_slots = lax.all_gather(slot_factor, "day", axis=0, tiled=True)
    features = (day_factor[:, None, :] * all_slots[None, :, :]).reshape(-1, rank)
    row_total = features.shape[0] * lax.axis_size("day")
    outer_rows = (features[:, :, None] * features[:, None, :]).reshape(-1, rank * rank)
    mask_half = observed.astype(jnp.bfloat16)
    weighted = mask_half * y_obs
    dims = (((0,), (0,)), ((), ()))
    gram_sums = lax.dot_general(outer_rows, mask_half, dims, preferred_element_type=jnp.float32)
    right_sums = lax.dot_general(features, weighted, dims, preferred_element_type=jnp.float32)
    pieces = []
    for offset in (2, 1, 0, -1, -2):
        if offset == 0:
            pieces.append(sensor_factor)
        else:
            pieces.append(shifted(sensor_factor, "sensor", offset))
    window = jnp.concatenate(pieces, axis=1)
    base_col = (lax.axis_index("sensor") - 2) * block_len
    columns = neighbours - base_col
    picked = jnp.take(window, columns, axis=1).astype(jnp.float32)
    pulled = jnp.einsum("rns,ns->rs", picked, edge_weight)
    prior_diag = 1.0 + jnp.sum(edge_weight, axis=0)
    tau = 4.0 / row_total
    sums = jnp.concatenate([gram_sums, right_sums], axis=0)
    sums = lax.psum_scatter(sums, "day", scatter_dimension=1, tiled=True)
    share_len = sums.shape[1]
    first_col = lax.axis_index("day") * share_len
    part = lambda array: lax.dynamic_slice_in_dim(array, first_col, share_len, array.ndim - 1)
    solved = solve_block(
        sums[: rank * rank].reshape(rank, rank, share_len),
        sums[rank * rank :],
        part(pulled),
        part(prior_diag),
        prior_scale,
        part(noise),
        tau,
    )
    return lax.all_gather(solved, "day", axis=1, tiled=True)


COUNTS = [4 - block // 2 for block in range(BLOCKS)]
STARTS = [64 * sum(COUNTS[:block]) for block in range(BLOCKS)]
PACKED_ROWS = 64 * sum(COUNTS)
OFFSETS = (-2, -1, 1, 2)


def pack_pair(even, odd, own):
    low = lane_low(even.shape)
    if own:
        return jnp.where(low, even, pltpu.roll(odd, HALF, 1))
    return jnp.where(low, pltpu.roll(even, HALF, 1), odd)


def split_pairs(rows):
    count = rows.shape[0] // 16
    pairs = rows.reshape(count, 2, 8, LANES)
    return pairs[:, 0].reshape(8 * count, LANES), pairs[:, 1].reshape(8 * count, LANES)


def sweep_kernel(
    tau,
    days,
    y_hbm,
    observed_hbm,
    day_ref,
    slot_ref,
    factor_ref,
    scale_ref,
    neighbour_ref,
    weight_ref,
    noise_ref,
    out_ref,
    y_ref,
    observed_ref,
    mask_ref,
    weighted_ref,
    peer_slots,
    window,
    features,
    wide_features,
    half_features,
    outer,
    own_gram,
    sent_gram,
    got_gram,
    own_right,
    sent_right,
    got_right,
    pulled_ref,
    prior_ref,
    noise_own,
    packed_ref,
    peer_packed,
    found,
    cols,
    wide,
    inv_diag,
    halfway,
    load_sems,
    slot_sems,
    window_send,
    window_recv,
    gram_send,
    gram_recv,
    right_sems,
    final_sems,
):
    day = lax.axis_index("day")
    sensor = lax.axis_index("sensor")
    sensors = lax.axis_size("sensor")
    rows = y_ref.shape[0]
    padded = mask_ref.shape[0]
    half_slots = slot_ref.shape[0]
    peer = {"day": 1 - day}
    mesh_id = pl.DeviceIdType.MESH

    load_mask = pltpu.make_async_copy(observed_hbm, observed_ref, load_sems.at[0])
    load_y = pltpu.make_async_copy(y_hbm, y_ref, load_sems.at[1])
    load_mask.start()
    load_y.start()
    barrier = pltpu.get_barrier_semaphore()
    pl.semaphore_signal(barrier, inc=1, device_id=peer, device_id_type=mesh_id)
    others = [lax.rem(sensor + sensors + offset, sensors) for offset in OFFSETS]
    for other in others:
        pl.semaphore_signal(barrier, inc=1, device_id={"sensor": other}, device_id_type=mesh_id)
    pl.semaphore_wait(barrier, 1 + len(OFFSETS))

    def to_peer(source, target, send, recv):
        return pltpu.make_async_remote_copy(
            src_ref=source,
            dst_ref=target,
            send_sem=send,
            recv_sem=recv,
            device_id=peer,
            device_id_type=mesh_id,
        )

    slot_copy = to_peer(slot_ref, peer_slots, slot_sems.at[0], slot_sems.at[1])
    slot_copy.start()
    window_copies = []
    for index, (offset, other) in enumerate(zip(OFFSETS, others)):
        copy = pltpu.make_async_remote_copy(
            src_ref=factor_ref,
            dst_ref=window.at[2 - offset],
            send_sem=window_send.at[index],
            recv_sem=window_recv.at[index],
            device_id={"sensor": other},
            device_id_type=mesh_id,
        )
        copy.start()
        window_copies.append(copy)

    def own_first(tile):
        return jnp.where(day == 0, tile, pltpu.roll(tile, HALF, 1))

    load_mask.wait()
    mask = own_first(observed_ref[...].astype(jnp.float32))
    mask_ref[pl.ds(0, rows), :] = mask.astype(jnp.bfloat16)
    load_y.wait()
    readings = own_first(y_ref[...].astype(jnp.float32))
    weighted_ref[pl.ds(0, rows), :] = (mask * readings).astype(jnp.bfloat16)
    if padded > rows:
        empty = jnp.zeros((padded - rows, LANES), jnp.bfloat16)
        mask_ref[pl.ds(rows, padded - rows), :] = empty
        weighted_ref[pl.ds(rows, padded - rows), :] = empty
        features[pl.ds(rows, padded - rows), :] = jnp.zeros((padded - rows, LANES), jnp.float32)

    mine = (lax.broadcasted_iota(jnp.int32, (RANK, LANES), 1) >= HALF) == (day == 1)

    def spread_own(tile):
        return jnp.where(mine, tile, pltpu.roll(tile, HALF, 1))

    eye_rows = lax.broadcasted_iota(jnp.int32, (RANK, RANK), 0)
    eye_cols = lax.broadcasted_iota(jnp.int32, (RANK, RANK), 1)
    scale_row = jnp.broadcast_to(scale_ref[...], (RANK, RANK))
    scale = jnp.sum(jnp.where(eye_rows == eye_cols, scale_row, 0.0), axis=1, keepdims=True)
    scale = jnp.broadcast_to(scale, (RANK, LANES))
    prior_diag = 1.0 + jnp.sum(weight_ref[...], axis=0, keepdims=True)
    prior_ref[...] = scale * spread_own(jnp.broadcast_to(prior_diag, (RANK, LANES)))
    noise_own[...] = spread_own(noise_ref[...])

    slot_copy.wait()
    here = slot_ref[...].astype(jnp.float32)
    there = peer_slots[...].astype(jnp.float32)
    here = jnp.concatenate([here, here], axis=1)
    there = jnp.concatenate([there, there], axis=1)
    early = jnp.where(day == 0, here, there)
    late = jnp.where(day == 0, there, here)
    day_rows = day_ref[...].astype(jnp.float32)
    day_rows = jnp.concatenate([day_rows, day_rows], axis=1)
    for index in range(days):
        row = day_rows[index : index + 1, :]
        base = index * 2 * half_slots
        features[pl.ds(base, half_slots), :] = early * row
        features[pl.ds(base + half_slots, half_slots), :] = late * row
    for index in range(padded // LANES):
        piece = features[pl.ds(index * LANES, LANES), :].T[:RANK]
        rounded = piece.astype(jnp.bfloat16)
        half_features[:, pl.ds(index * LANES, LANES)] = rounded
        wide_features[:, pl.ds(index * LANES, LANES)] = rounded.astype(jnp.float32)

    right = jnp.dot(half_features[...], weighted_ref[...], preferred_element_type=jnp.float32)
    even, odd = split_pairs(right)
    own_right[...] = pack_pair(even, odd, True)
    sent_right[...] = pack_pair(even, odd, False)
    right_copy = to_peer(sent_right, got_right, right_sems.at[0], right_sems.at[1])
    right_copy.start()

    gram_copies = []
    for block in range(BLOCKS):
        first = block // 2
        count = COUNTS[block]
        slab = outer.at[block % 2]
        for c in range(8):
            row = wide_features[pl.ds(8 * block + c, 1), :]
            row = jnp.broadcast_to(row, (16, padded)).astype(jnp.bfloat16)
            for q in range(first, 4):
                at = 16 * (c * count + q - first)
                slab[pl.ds(at, 16), :] = half_features[pl.ds(16 * q, 16), :] * row
        sums = jnp.dot(
            slab[pl.ds(0, 128 * count), :], mask_ref[...], preferred_element_type=jnp.float32
        )
        even, odd = split_pairs(sums)
        part = pl.ds(STARTS[block], 64 * count)
        sent_gram[part, :] = pack_pair(even, odd, False).astype(sent_gram.dtype)
        copy = to_peer(
            sent_gram.at[part], got_gram.at[part], gram_send.at[block], gram_recv.at[block]
        )
        copy.start()
        own_gram[part, :] = pack_pair(even, odd, True)
        gram_copies.append(copy)

    base = (sensor - 2) * LANES
    column = neighbour_ref[...] - base
    weights = weight_ref[...]
    pulled = jnp.zeros((RANK, LANES), jnp.float32)
    for copy in window_copies:
        copy.wait()
    for slot in range(5):
        ids = lax.broadcasted_iota(jnp.int32, (LANES, LANES), 0) + slot * LANES
        picks = jnp.zeros((LANES, LANES), jnp.float32)
        for n in range(neighbour_ref.shape[0]):
            picks = picks + jnp.where(ids == column[n : n + 1, :], weights[n : n + 1, :], 0.0)
        high = picks.astype(jnp.bfloat16)
        low_part = (picks - high.astype(jnp.float32)).astype(jnp.bfloat16)
        source = factor_ref[...] if slot == 2 else window[slot]
        pulled = pulled + jnp.dot(source, high, preferred_element_type=jnp.float32)
        pulled = pulled + jnp.dot(source, low_part, preferred_element_type=jnp.float32)
    pulled = scale * spread_own(pulled)
    even, odd = split_pairs(pulled)
    right_copy.wait()
    target = tau * (own_right[...] + got_right[...])
    target = target + jnp.where(lane_low(even.shape), even, odd)

    def load_columns(block):
        first = block // 2
        count = COUNTS[block]
        gram_copies[block].wait_recv()
        prior = prior_ref[pl.ds(8 * block, 8), :]
        columns = []
        for c in range(8):
            tiles = []
            for q in range(first, 4):
                at = pl.ds(STARTS[block] + 8 * (c * count + q - first), 8)
                tiles.append(tau * (own_gram[at, :] + got_gram[at, :].astype(jnp.float32)))
            tiles[0] = tiles[0] + diagonal_tile(block, c, prior)
            columns.append(tiles)
        return columns

    packed = factor_and_solve(
        load_columns,
        [target[8 * q : 8 * q + 8, :] for q in range(4)],
        lambda block: noise_own[pl.ds(8 * block, 8), :],
        cols,
        wide,
        inv_diag,
        halfway,
        found,
    )
    for q in range(4):
        packed_ref[pl.ds(8 * q, 8), :] = packed[q]
    final_copy = to_peer(packed_ref, peer_packed, final_sems.at[0], final_sems.at[1])
    final_copy.start()
    for copy in gram_copies:
        copy.wait_send()
    final_copy.wait()
    mine_tile = (lax.broadcasted_iota(jnp.int32, (8, LANES), 1) >= HALF) == (day == 1)
    for tile in range(8):
        theirs = both_halves(peer_packed[pl.ds(8 * (tile // 2), 8), :], tile % 2 == 1)
        at = pl.ds(8 * tile, 8)
        out_ref[at, :] = jnp.where(mine_tile, found[at, :], theirs)


def paired_shards(
    y_obs,
    observed,
    day_factor,
    slot_factor,
    sensor_factor,
    prior_scale,
    neighbours,
    edge_weight,
    noise,
):
    rows = y_obs.shape[0]
    padded = -(-rows // 256) * 256
    half_slots = slot_factor.shape[0]
    days = day_factor.shape[0]
    tau = 4.0 / (2 * rows)
    vmem = pl.BlockSpec(memory_space=pltpu.VMEM)
    hbm = pl.BlockSpec(memory_space=pl.ANY)
    f32, bf16 = jnp.float32, jnp.bfloat16
    dma = pltpu.SemaphoreType.DMA
    return pl.pallas_call(
        functools.partial(sweep_kernel, tau, days),
        out_shape=jax.ShapeDtypeStruct((RANK, LANES), f32),
        in_specs=[hbm, hbm] + [vmem] * 7,
        out_specs=vmem,
        scratch_shapes=[
            pltpu.VMEM((rows, LANES), bf16),
            pltpu.VMEM((rows, LANES), jnp.int32),
            pltpu.VMEM((padded, LANES), bf16),
            pltpu.VMEM((padded, LANES), bf16),
            pltpu.VMEM((half_slots, RANK), bf16),
            pltpu.VMEM((5, RANK, LANES), bf16),
            pltpu.VMEM((padded, LANES), f32),
            pltpu.VMEM((RANK, padded), f32),
            pltpu.VMEM((RANK, padded), bf16),
            pltpu.VMEM((2, 512, padded), bf16),
            pltpu.VMEM((PACKED_ROWS, LANES), f32),
            pltpu.VMEM((PACKED_ROWS, LANES), f32),
            pltpu.VMEM((PACKED_ROWS, LANES), f32),
            pltpu.VMEM((32, LANES), f32),
            pltpu.VMEM((32, LANES), f32),
            pltpu.VMEM((32, LANES), f32),
            pltpu.VMEM((RANK, LANES), f32),
            pltpu.VMEM((RANK, LANES), f32),
            pltpu.VMEM((RANK, LANES), f32),
            pltpu.VMEM((32, LANES), f32),
            pltpu.VMEM((32, LANES), f32),
            pltpu.VMEM((RANK, LANES), f32),
        ]
        + solver_scratch()
        + [dma((2,)), dma((2,)), dma((4,)), dma((4,)), dma((8,)), dma((8,)), dma((2,)), dma((2,))],
        compiler_params=pltpu.CompilerParams(
            collective_id=0, has_side_effects=True, vmem_limit_bytes=40 * 1024 * 1024
        ),
        name="sweep_sensors",
    )(
        y_obs,
        observed,
        day_factor,
        slot_factor,
        sensor_factor,
        prior_scale.reshape(1, RANK),
        neighbours,
        edge_weight,
        noise,
    )


def solution(mesh):
    sizes = dict(mesh.shape)

    def shards(*arrays):
        y_obs, slot_factor = arrays[0], arrays[3]
        fits = sizes["day"] == 2 and sizes["sensor"] >= 5 and y_obs.shape[1] == LANES
        fits = fits and y_obs.shape[0] % 16 == 0 and slot_factor.shape[0] % 16 == 0
        return paired_shards(*arrays) if fits else general_shards(*arrays)

    return jax.shard_map(
        shards,
        mesh=mesh,
        in_specs=(
            P("day", "sensor"),
            P("day", "sensor"),
            P("day", None),
            P("day", None),
            P(None, "sensor"),
            P(),
            P(None, "sensor"),
            P(None, "sensor"),
            P(None, "sensor"),
        ),
        out_specs=P(None, "sensor"),
        check_vma=False,
    )
```

```python
import functools

import jax
import jax.numpy as jnp
from jax import lax
from jax.experimental import pallas as pl
from jax.experimental.pallas import tpu as pltpu
from jax.sharding import PartitionSpec as P

RANK = 64
LANES = 128
HALF = 64
BLOCKS = RANK // 8
VMEM_BYTES = 62 * 1024 * 1024


def lane_low(shape):
    return lax.broadcasted_iota(jnp.int32, shape, len(shape) - 1) < HALF


def both_halves(tile, upper):
    other = pltpu.roll(tile, HALF, 1)
    low = lane_low(tile.shape)
    return jnp.where(low, other, tile) if upper else jnp.where(low, tile, other)


def row_of(tile, index):
    return jnp.broadcast_to(tile[index : index + 1, :], tile.shape)


def factor_and_solve(load_columns, target, noise_tile, cols, wide, inv_diag, halfway, found):
    target = list(target)
    for block in range(BLOCKS):
        first = block // 2
        upper = block % 2 == 1
        count = 4 - first
        columns = load_columns(block)
        if block > 0:

            def subtract(k, carry):
                done = [cols[k, pl.ds(8 * q, 8), :] for q in range(first, 4)]
                out = []
                for c in range(8):
                    scale = jnp.broadcast_to(wide[k, pl.ds(8 * block + c, 1), :], (8, LANES))
                    out.extend(carry[c * count + q] - done[q] * scale for q in range(count))
                return tuple(out)

            flat = tuple(tile for column in columns for tile in column)
            flat = lax.fori_loop(0, 8 * block, subtract, flat, unroll=2)
            columns = [list(flat[c * count : (c + 1) * count]) for c in range(8)]
        corner = [both_halves(column[0], upper) for column in columns]
        side = both_halves(target[first], upper)
        for c in range(8):
            j = 8 * block + c
            inverse = lax.rsqrt(row_of(corner[c], c))
            corner[c] = corner[c] * inverse
            columns[c] = [tile * inverse for tile in columns[c]]
            solved = row_of(side, c) * inverse
            side = side - corner[c] * solved
            for q in range(count):
                target[first + q] = target[first + q] - columns[c][q] * solved
            for later in range(c + 1, 8):
                scale = row_of(corner[c], later)
                corner[later] = corner[later] - corner[c] * scale
                columns[later] = [
                    tile - own * scale for tile, own in zip(columns[later], columns[c])
                ]
            inv_diag[j] = inverse
            halfway[pl.ds(j, 1), :] = solved[0:1, :]
        for c in range(8):
            j = 8 * block + c
            for q in range(count):
                tile = columns[c][q]
                row = 16 * (first + q)
                cols[j, pl.ds(8 * (first + q), 8), :] = tile
                if row >= 8 * block:
                    wide[j, pl.ds(row, 8), :] = both_halves(tile, False)
                wide[j, pl.ds(row + 8, 8), :] = both_halves(tile, True)

    packed = [None] * 4
    low = lane_low((8, LANES))
    below = None
    for block in reversed(range(BLOCKS)):
        first = block // 2
        upper = block % 2 == 1
        right = halfway[pl.ds(8 * block, 8), :] + noise_tile(block)
        remain = []
        for c in range(8):
            j = 8 * block + c
            total = row_of(right, c)
            parts = None
            for q in range(first, 4):
                if q == first and upper:
                    continue
                if q == first:
                    term = jnp.where(low, 0.0, cols[j, pl.ds(8 * q, 8), :] * below)
                else:
                    term = cols[j, pl.ds(8 * q, 8), :] * packed[q]
                parts = term if parts is None else parts + term
            if parts is not None:
                sums = jnp.sum(parts, axis=0, keepdims=True)
                sums = jnp.broadcast_to(sums, (8, LANES))
                total = total - (sums + pltpu.roll(sums, HALF, 1))
            remain.append(total)
        values = [None] * 8
        for c in reversed(range(8)):
            values[c] = remain[c] * inv_diag[8 * block + c]
            for earlier in range(c):
                scale = jnp.broadcast_to(
                    wide[8 * block + earlier, pl.ds(8 * block + c, 1), :], (8, LANES)
                )
                remain[earlier] = remain[earlier] - scale * values[c]
        rows = lax.broadcasted_iota(jnp.int32, (8, LANES), 0)
        tile = values[0]
        for c in range(1, 8):
            tile = jnp.where(rows == c, values[c], tile)
        found[pl.ds(8 * block, 8), :] = tile
        if upper:
            below = tile
        else:
            packed[first] = jnp.where(low, tile, below)
            below = None
    return packed


def diagonal_tile(block, c, value):
    shape = (8, LANES)
    rows = lax.broadcasted_iota(jnp.int32, shape, 0)
    low = lane_low(shape)
    half = low if block % 2 == 0 else jnp.logical_not(low)
    return jnp.where((rows == c) & half, value, 0.0)


def solve_kernel(squares, target, noise, prior, out, cols, wide, inv_diag, halfway):
    def load_columns(block):
        first = block // 2
        own = prior[pl.ds(8 * block, 8), :]
        columns = []
        for c in range(8):
            j = 8 * block + c
            tiles = [squares[j, pl.ds(8 * q, 8), :] for q in range(first, 4)]
            tiles[0] = tiles[0] + diagonal_tile(block, c, own)
            columns.append(tiles)
        return columns

    targets = [target[pl.ds(8 * q, 8), :] for q in range(4)]
    factor_and_solve(
        load_columns,
        targets,
        lambda block: noise[pl.ds(8 * block, 8), :],
        cols,
        wide,
        inv_diag,
        halfway,
        out,
    )


def solver_scratch():
    return [
        pltpu.VMEM((RANK, 32, LANES), jnp.float32),
        pltpu.VMEM((RANK, RANK, LANES), jnp.float32),
        pltpu.VMEM((RANK, 8, LANES), jnp.float32),
        pltpu.VMEM((RANK, LANES), jnp.float32),
    ]


def pack_rows(rows):
    lead = rows.shape[:-2]
    split = rows.reshape(lead + (4, 2, 8, HALF))
    return jnp.swapaxes(split, -3, -2).reshape(lead + (32, LANES))


def solve_block(gram, right, pulled, prior_diag, prior_scale, noise, tau):
    share = right.shape[1]

    def fill(array, value=0.0):
        pad = [(0, 0)] * (array.ndim - 1) + [(0, HALF - share)]
        return jnp.pad(array, pad, constant_values=value)

    target = tau * right + prior_scale[:, None] * pulled
    prior = prior_scale[:, None] * fill(prior_diag, 1.0)[None, :]
    twice = lambda array: jnp.concatenate([array, array], axis=1)
    spec = pl.BlockSpec(memory_space=pltpu.VMEM)
    solved = pl.pallas_call(
        solve_kernel,
        out_shape=jax.ShapeDtypeStruct((RANK, LANES), jnp.float32),
        in_specs=[spec] * 4,
        out_specs=spec,
        scratch_shapes=solver_scratch(),
        compiler_params=pltpu.CompilerParams(vmem_limit_bytes=24 * 1024 * 1024),
        name="solve_sensors",
    )(tau * pack_rows(fill(gram)), pack_rows(fill(target)), twice(fill(noise)), twice(prior))
    return solved[:, :share]


def shifted(shard, axis, by):
    size = lax.axis_size(axis)
    pairs = [(i, i + by) for i in range(size) if 0 <= i + by < size]
    return lax.ppermute(shard, axis, pairs)


def general_shards(
    y_obs,
    observed,
    day_factor,
    slot_factor,
    sensor_factor,
    prior_scale,
    neighbours,
    edge_weight,
    noise,
):
    rank = sensor_factor.shape[0]
    block_len = sensor_factor.shape[1]
    all_slots = lax.all_gather(slot_factor, "day", axis=0, tiled=True)
    features = (day_factor[:, None, :] * all_slots[None, :, :]).reshape(-1, rank)
    row_total = features.shape[0] * lax.axis_size("day")
    outer_rows = (features[:, :, None] * features[:, None, :]).reshape(-1, rank * rank)
    mask_half = observed.astype(jnp.bfloat16)
    weighted = mask_half * y_obs
    dims = (((0,), (0,)), ((), ()))
    gram_sums = lax.dot_general(outer_rows, mask_half, dims, preferred_element_type=jnp.float32)
    right_sums = lax.dot_general(features, weighted, dims, preferred_element_type=jnp.float32)
    pieces = []
    for offset in (2, 1, 0, -1, -2):
        if offset == 0:
            pieces.append(sensor_factor)
        else:
            pieces.append(shifted(sensor_factor, "sensor", offset))
    window = jnp.concatenate(pieces, axis=1)
    base_col = (lax.axis_index("sensor") - 2) * block_len
    columns = neighbours - base_col
    picked = jnp.take(window, columns, axis=1).astype(jnp.float32)
    pulled = jnp.einsum("rns,ns->rs", picked, edge_weight)
    prior_diag = 1.0 + jnp.sum(edge_weight, axis=0)
    tau = 4.0 / row_total
    sums = jnp.concatenate([gram_sums, right_sums], axis=0)
    sums = lax.psum_scatter(sums, "day", scatter_dimension=1, tiled=True)
    share_len = sums.shape[1]
    first_col = lax.axis_index("day") * share_len
    part = lambda array: lax.dynamic_slice_in_dim(array, first_col, share_len, array.ndim - 1)
    solved = solve_block(
        sums[: rank * rank].reshape(rank, rank, share_len),
        sums[rank * rank :],
        part(pulled),
        part(prior_diag),
        prior_scale,
        part(noise),
        tau,
    )
    return lax.all_gather(solved, "day", axis=1, tiled=True)


COUNTS = [4 - block // 2 for block in range(BLOCKS)]
STARTS = [64 * sum(COUNTS[:block]) for block in range(BLOCKS)]
PACKED_ROWS = 64 * sum(COUNTS)
OFFSETS = (-2, -1, 1, 2)
DAY_ROWS = 16


def pack_pair(even, odd, own):
    low = lane_low(even.shape)
    if own:
        return jnp.where(low, even, pltpu.roll(odd, HALF, 1))
    return jnp.where(low, pltpu.roll(even, HALF, 1), odd)


def split_pairs(rows):
    count = rows.shape[0] // 16
    pairs = rows.reshape(count, 2, 8, LANES)
    return pairs[:, 0].reshape(8 * count, LANES), pairs[:, 1].reshape(8 * count, LANES)


def sweep_kernel(
    tau,
    days,
    y_hbm,
    observed_hbm,
    day_ref,
    slot_ref,
    factor_ref,
    scale_ref,
    neighbour_ref,
    weight_ref,
    noise_ref,
    out_ref,
    y_ref,
    observed_ref,
    mask_ref,
    weighted_ref,
    sent_mask,
    got_mask,
    sent_weighted,
    got_weighted,
    slot_wide,
    sent_factors,
    got_factors,
    window,
    features,
    wide_features,
    half_features,
    outer,
    gram,
    prior_ref,
    noise_own,
    packed_ref,
    peer_packed,
    found,
    cols,
    wide,
    inv_diag,
    halfway,
    load_sems,
    factor_sems,
    mask_sems,
    weighted_sems,
    window_send,
    window_recv,
    final_sems,
):
    day = lax.axis_index("day")
    sensor = lax.axis_index("sensor")
    sensors = lax.axis_size("sensor")
    rows = y_ref.shape[0]
    half_rows = rows // 2
    padded = mask_ref.shape[1]
    half_slots = slot_ref.shape[1]
    peer = {"day": 1 - day}
    mesh_id = pl.DeviceIdType.MESH
    f32, bf16 = jnp.float32, jnp.bfloat16

    load_mask = pltpu.make_async_copy(observed_hbm, observed_ref, load_sems.at[0])
    load_y = pltpu.make_async_copy(y_hbm, y_ref, load_sems.at[1])
    load_mask.start()
    load_y.start()
    barrier = pltpu.get_barrier_semaphore()
    pl.semaphore_signal(barrier, inc=1, device_id=peer, device_id_type=mesh_id)
    others = [lax.rem(sensor + sensors + offset, sensors) for offset in OFFSETS]
    for other in others:
        pl.semaphore_signal(barrier, inc=1, device_id={"sensor": other}, device_id_type=mesh_id)

    def to_peer(source, target, sems):
        return pltpu.make_async_remote_copy(
            src_ref=source,
            dst_ref=target,
            send_sem=sems.at[0],
            recv_sem=sems.at[1],
            device_id=peer,
            device_id_type=mesh_id,
        )

    slot_wide[...] = jnp.zeros(slot_wide.shape, f32)
    slot_wide[pl.ds(0, RANK), pl.ds(0, half_slots)] = slot_ref[...].astype(f32)
    here = slot_wide[...].T[:half_slots]
    sent_factors[pl.ds(0, half_slots), :] = here.astype(bf16)
    day_own = day_ref[...].astype(f32)
    day_own = jnp.concatenate([day_own, day_own], axis=1)
    tile_rows = lax.broadcasted_iota(jnp.int32, (DAY_ROWS, LANES), 0)
    day_tile = jnp.zeros((DAY_ROWS, LANES), f32)
    for index in range(days):
        day_tile = jnp.where(tile_rows == index, day_own[index : index + 1, :], day_tile)
    sent_factors[pl.ds(half_slots, DAY_ROWS), :] = day_tile.astype(bf16)

    def own_first(tile):
        return jnp.where(day == 0, tile, pltpu.roll(tile, HALF, 1))

    load_mask.wait()
    mask = own_first(observed_ref[...].astype(f32))
    mask_ref[0, pl.ds(0, rows), :] = mask.astype(bf16)
    sent_mask[...] = pack_pair(mask[:half_rows], mask[half_rows:], False).astype(bf16)

    pl.semaphore_wait(barrier, 1 + len(OFFSETS))
    factor_copy = to_peer(sent_factors, got_factors, factor_sems)
    factor_copy.start()
    mask_copy = to_peer(sent_mask, got_mask, mask_sems)
    mask_copy.start()
    window_copies = []
    for index, (offset, other) in enumerate(zip(OFFSETS, others)):
        copy = pltpu.make_async_remote_copy(
            src_ref=factor_ref,
            dst_ref=window.at[2 - offset],
            send_sem=window_send.at[index],
            recv_sem=window_recv.at[index],
            device_id={"sensor": other},
            device_id_type=mesh_id,
        )
        copy.start()
        window_copies.append(copy)

    load_y.wait()
    weighted = own_first(observed_ref[...].astype(f32) * y_ref[...].astype(f32))
    weighted_ref[0, pl.ds(0, rows), :] = weighted.astype(bf16)
    sent_weighted[...] = pack_pair(weighted[:half_rows], weighted[half_rows:], False).astype(bf16)
    weighted_copy = to_peer(sent_weighted, got_weighted, weighted_sems)
    weighted_copy.start()
    if padded > rows:
        empty = jnp.zeros((padded - rows, LANES), bf16)
        for part in range(2):
            mask_ref[part, pl.ds(rows, padded - rows), :] = empty
            weighted_ref[part, pl.ds(rows, padded - rows), :] = empty
        features[pl.ds(rows, padded - rows), :] = jnp.zeros((padded - rows, LANES), f32)

    factor_copy.wait()
    there = got_factors[pl.ds(0, half_slots), :].astype(f32)
    early = jnp.where(day == 0, here, there)
    late = jnp.where(day == 0, there, here)
    day_peer = got_factors[pl.ds(half_slots, DAY_ROWS), :].astype(f32)

    def make_features(part):
        day_rows = day_own if part == 0 else day_peer
        for index in range(days):
            row = day_rows[index : index + 1, :]
            at = index * 2 * half_slots
            features[pl.ds(at, half_slots), :] = early * row
            features[pl.ds(at + half_slots, half_slots), :] = late * row
        for index in range(padded // LANES):
            piece = features[pl.ds(index * LANES, LANES), :].T[:RANK]
            rounded = piece.astype(bf16)
            half_features[part, :, pl.ds(index * LANES, LANES)] = rounded
            wide_features[part, :, pl.ds(index * LANES, LANES)] = rounded.astype(f32)

    def gram_block(part, block):
        first = block // 2
        count = COUNTS[block]
        slab = outer.at[block % 2]
        for c in range(8):
            row = wide_features[part, pl.ds(8 * block + c, 1), :]
            row = jnp.broadcast_to(row, (16, padded)).astype(bf16)
            for q in range(first, 4):
                at = 16 * (c * count + q - first)
                slab[pl.ds(at, 16), :] = half_features[part, pl.ds(16 * q, 16), :] * row
        sums = jnp.dot(slab[pl.ds(0, 128 * count), :], mask_ref[part], preferred_element_type=f32)
        even, odd = split_pairs(sums)
        return pack_pair(even, odd, True)

    make_features(0)
    for block in range(BLOCKS):
        gram[pl.ds(STARTS[block], 64 * COUNTS[block]), :] = gram_block(0, block)
    make_features(1)

    mine = (lax.broadcasted_iota(jnp.int32, (RANK, LANES), 1) >= HALF) == (day == 1)

    def spread_own(tile):
        return jnp.where(mine, tile, pltpu.roll(tile, HALF, 1))

    eye_rows = lax.broadcasted_iota(jnp.int32, (RANK, RANK), 0)
    eye_cols = lax.broadcasted_iota(jnp.int32, (RANK, RANK), 1)
    scale_row = jnp.broadcast_to(scale_ref[...], (RANK, RANK))
    scale = jnp.sum(jnp.where(eye_rows == eye_cols, scale_row, 0.0), axis=1, keepdims=True)
    scale = jnp.broadcast_to(scale, (RANK, LANES))
    prior_diag = 1.0 + jnp.sum(weight_ref[...], axis=0, keepdims=True)
    prior_ref[...] = scale * spread_own(jnp.broadcast_to(prior_diag, (RANK, LANES)))
    noise_own[...] = spread_own(noise_ref[...])

    base = (sensor - 2) * LANES
    column = neighbour_ref[...] - base
    weights = weight_ref[...]
    pulled = jnp.zeros((RANK, LANES), f32)
    for copy in window_copies:
        copy.wait()
    for slot in range(5):
        ids = lax.broadcasted_iota(jnp.int32, (LANES, LANES), 0) + slot * LANES
        picks = jnp.zeros((LANES, LANES), f32)
        for n in range(neighbour_ref.shape[0]):
            picks = picks + jnp.where(ids == column[n : n + 1, :], weights[n : n + 1, :], 0.0)
        high = picks.astype(bf16)
        low_part = (picks - high.astype(f32)).astype(bf16)
        source = factor_ref[...] if slot == 2 else window[slot]
        pulled = pulled + jnp.dot(source, high, preferred_element_type=f32)
        pulled = pulled + jnp.dot(source, low_part, preferred_element_type=f32)
    pulled = scale * spread_own(pulled)
    even, odd = split_pairs(pulled)
    pulled = jnp.where(lane_low(even.shape), even, odd)

    def unpack(packed, target):
        target[1, pl.ds(0, half_rows), :] = packed[...]
        turned = pltpu.roll(packed[...].astype(f32), HALF, 1)
        target[1, pl.ds(half_rows, half_rows), :] = turned.astype(bf16)

    mask_copy.wait()
    unpack(got_mask, mask_ref)
    for block in range(BLOCKS):
        at = pl.ds(STARTS[block], 64 * COUNTS[block])
        gram[at, :] = tau * (gram[at, :] + gram_block(1, block))

    weighted_copy.wait()
    unpack(got_weighted, weighted_ref)
    right = jnp.dot(half_features[0], weighted_ref[0], preferred_element_type=f32)
    right = right + jnp.dot(half_features[1], weighted_ref[1], preferred_element_type=f32)
    even, odd = split_pairs(right)
    target = tau * pack_pair(even, odd, True) + pulled

    def load_columns(block):
        first = block // 2
        count = COUNTS[block]
        prior = prior_ref[pl.ds(8 * block, 8), :]
        columns = []
        for c in range(8):
            tiles = []
            for q in range(first, 4):
                tiles.append(gram[pl.ds(STARTS[block] + 8 * (c * count + q - first), 8), :])
            tiles[0] = tiles[0] + diagonal_tile(block, c, prior)
            columns.append(tiles)
        return columns

    packed = factor_and_solve(
        load_columns,
        [target[8 * q : 8 * q + 8, :] for q in range(4)],
        lambda block: noise_own[pl.ds(8 * block, 8), :],
        cols,
        wide,
        inv_diag,
        halfway,
        found,
    )
    for q in range(4):
        packed_ref[pl.ds(8 * q, 8), :] = packed[q]
    final_copy = to_peer(packed_ref, peer_packed, final_sems)
    final_copy.start()
    final_copy.wait()
    mine_tile = (lax.broadcasted_iota(jnp.int32, (8, LANES), 1) >= HALF) == (day == 1)
    for tile in range(8):
        theirs = both_halves(peer_packed[pl.ds(8 * (tile // 2), 8), :], tile % 2 == 1)
        at = pl.ds(8 * tile, 8)
        out_ref[at, :] = jnp.where(mine_tile, found[at, :], theirs)


def paired_shards(
    y_obs,
    observed,
    day_factor,
    slot_factor,
    sensor_factor,
    prior_scale,
    neighbours,
    edge_weight,
    noise,
):
    rows = y_obs.shape[0]
    padded = -(-rows // 256) * 256
    half_slots = slot_factor.shape[0]
    slot_lanes = -(-half_slots // LANES) * LANES
    days = day_factor.shape[0]
    tau = 4.0 / (2 * rows)
    vmem = pl.BlockSpec(memory_space=pltpu.VMEM)
    hbm = pl.BlockSpec(memory_space=pl.ANY)
    f32, bf16 = jnp.float32, jnp.bfloat16
    dma = pltpu.SemaphoreType.DMA
    return pl.pallas_call(
        functools.partial(sweep_kernel, tau, days),
        out_shape=jax.ShapeDtypeStruct((RANK, LANES), f32),
        in_specs=[hbm, hbm] + [vmem] * 7,
        out_specs=vmem,
        scratch_shapes=[
            pltpu.VMEM((rows, LANES), bf16),
            pltpu.VMEM((rows, LANES), jnp.int32),
            pltpu.VMEM((2, padded, LANES), bf16),
            pltpu.VMEM((2, padded, LANES), bf16),
            pltpu.VMEM((rows // 2, LANES), bf16),
            pltpu.VMEM((rows // 2, LANES), bf16),
            pltpu.VMEM((rows // 2, LANES), bf16),
            pltpu.VMEM((rows // 2, LANES), bf16),
            pltpu.VMEM((LANES, slot_lanes), f32),
            pltpu.VMEM((half_slots + DAY_ROWS, LANES), bf16),
            pltpu.VMEM((half_slots + DAY_ROWS, LANES), bf16),
            pltpu.VMEM((5, RANK, LANES), bf16),
            pltpu.VMEM((padded, LANES), f32),
            pltpu.VMEM((2, RANK, padded), f32),
            pltpu.VMEM((2, RANK, padded), bf16),
            pltpu.VMEM((2, 512, padded), bf16),
            pltpu.VMEM((PACKED_ROWS, LANES), f32),
            pltpu.VMEM((RANK, LANES), f32),
            pltpu.VMEM((RANK, LANES), f32),
            pltpu.VMEM((32, LANES), f32),
            pltpu.VMEM((32, LANES), f32),
            pltpu.VMEM((RANK, LANES), f32),
        ]
        + solver_scratch()
        + [dma((2,)), dma((2,)), dma((2,)), dma((2,)), dma((4,)), dma((4,)), dma((2,))],
        compiler_params=pltpu.CompilerParams(
            collective_id=0, has_side_effects=True, vmem_limit_bytes=VMEM_BYTES
        ),
        name="sweep_sensors",
    )(
        y_obs,
        observed,
        day_factor,
        slot_factor.T,
        sensor_factor,
        prior_scale.reshape(1, RANK),
        neighbours,
        edge_weight,
        noise,
    )


def solution(mesh):
    sizes = dict(mesh.shape)

    def shards(*arrays):
        y_obs, slot_factor = arrays[0], arrays[3]
        fits = sizes["day"] == 2 and sizes["sensor"] >= 5 and y_obs.shape[1] == LANES
        fits = fits and y_obs.shape[0] % 32 == 0 and slot_factor.shape[0] % 16 == 0
        fits = fits and arrays[2].shape[0] <= DAY_ROWS
        return paired_shards(*arrays) if fits else general_shards(*arrays)

    return jax.shard_map(
        shards,
        mesh=mesh,
        in_specs=(
            P("day", "sensor"),
            P("day", "sensor"),
            P("day", None),
            P("day", None),
            P(None, "sensor"),
            P(),
            P(None, "sensor"),
            P(None, "sensor"),
            P(None, "sensor"),
        ),
        out_specs=P(None, "sensor"),
        check_vma=False,
    )
```

```python
import functools

import jax
import jax.numpy as jnp
from jax import lax
from jax.experimental import pallas as pl
from jax.experimental.pallas import tpu as pltpu
from jax.sharding import PartitionSpec as P

RANK = 64
LANES = 128
HALF = 64
BLOCKS = RANK // 8
VMEM_BYTES = 60 * 1024 * 1024


def lane_low(shape):
    return lax.broadcasted_iota(jnp.int32, shape, len(shape) - 1) < HALF


def both_halves(tile, upper):
    other = pltpu.roll(tile, HALF, 1)
    low = lane_low(tile.shape)
    return jnp.where(low, other, tile) if upper else jnp.where(low, tile, other)


def row_of(tile, index):
    return jnp.broadcast_to(tile[index : index + 1, :], tile.shape)


def factor_and_solve(load_columns, target, noise_tile, cols, wide, inv_diag, halfway, found):
    target = list(target)
    for block in range(BLOCKS):
        first = block // 2
        upper = block % 2 == 1
        count = 4 - first
        columns = load_columns(block)
        if block > 0:

            def subtract(k, carry):
                done = [cols[k, pl.ds(8 * q, 8), :] for q in range(first, 4)]
                out = []
                for c in range(8):
                    scale = jnp.broadcast_to(wide[k, pl.ds(8 * block + c, 1), :], (8, LANES))
                    out.extend(carry[c * count + q] - done[q] * scale for q in range(count))
                return tuple(out)

            flat = tuple(tile for column in columns for tile in column)
            flat = lax.fori_loop(0, 8 * block, subtract, flat, unroll=2)
            columns = [list(flat[c * count : (c + 1) * count]) for c in range(8)]
        corner = [both_halves(column[0], upper) for column in columns]
        side = both_halves(target[first], upper)
        for c in range(8):
            j = 8 * block + c
            inverse = lax.rsqrt(row_of(corner[c], c))
            corner[c] = corner[c] * inverse
            columns[c] = [tile * inverse for tile in columns[c]]
            solved = row_of(side, c) * inverse
            side = side - corner[c] * solved
            for q in range(count):
                target[first + q] = target[first + q] - columns[c][q] * solved
            for later in range(c + 1, 8):
                scale = row_of(corner[c], later)
                corner[later] = corner[later] - corner[c] * scale
                columns[later] = [
                    tile - own * scale for tile, own in zip(columns[later], columns[c])
                ]
            inv_diag[j] = inverse
            halfway[pl.ds(j, 1), :] = solved[0:1, :]
        for c in range(8):
            j = 8 * block + c
            for q in range(count):
                tile = columns[c][q]
                row = 16 * (first + q)
                cols[j, pl.ds(8 * (first + q), 8), :] = tile
                if row >= 8 * block:
                    wide[j, pl.ds(row, 8), :] = both_halves(tile, False)
                wide[j, pl.ds(row + 8, 8), :] = both_halves(tile, True)

    packed = [None] * 4
    low = lane_low((8, LANES))
    below = None
    for block in reversed(range(BLOCKS)):
        first = block // 2
        upper = block % 2 == 1
        right = halfway[pl.ds(8 * block, 8), :] + noise_tile(block)
        remain = []
        for c in range(8):
            j = 8 * block + c
            total = row_of(right, c)
            parts = None
            for q in range(first, 4):
                if q == first and upper:
                    continue
                if q == first:
                    term = jnp.where(low, 0.0, cols[j, pl.ds(8 * q, 8), :] * below)
                else:
                    term = cols[j, pl.ds(8 * q, 8), :] * packed[q]
                parts = term if parts is None else parts + term
            if parts is not None:
                sums = jnp.sum(parts, axis=0, keepdims=True)
                sums = jnp.broadcast_to(sums, (8, LANES))
                total = total - (sums + pltpu.roll(sums, HALF, 1))
            remain.append(total)
        values = [None] * 8
        for c in reversed(range(8)):
            values[c] = remain[c] * inv_diag[8 * block + c]
            for earlier in range(c):
                scale = jnp.broadcast_to(
                    wide[8 * block + earlier, pl.ds(8 * block + c, 1), :], (8, LANES)
                )
                remain[earlier] = remain[earlier] - scale * values[c]
        rows = lax.broadcasted_iota(jnp.int32, (8, LANES), 0)
        tile = values[0]
        for c in range(1, 8):
            tile = jnp.where(rows == c, values[c], tile)
        found[pl.ds(8 * block, 8), :] = tile
        if upper:
            below = tile
        else:
            packed[first] = jnp.where(low, tile, below)
            below = None
    return packed


def diagonal_tile(block, c, value):
    shape = (8, LANES)
    rows = lax.broadcasted_iota(jnp.int32, shape, 0)
    low = lane_low(shape)
    half = low if block % 2 == 0 else jnp.logical_not(low)
    return jnp.where((rows == c) & half, value, 0.0)


def solve_kernel(squares, target, noise, prior, out, cols, wide, inv_diag, halfway):
    def load_columns(block):
        first = block // 2
        own = prior[pl.ds(8 * block, 8), :]
        columns = []
        for c in range(8):
            j = 8 * block + c
            tiles = [squares[j, pl.ds(8 * q, 8), :] for q in range(first, 4)]
            tiles[0] = tiles[0] + diagonal_tile(block, c, own)
            columns.append(tiles)
        return columns

    targets = [target[pl.ds(8 * q, 8), :] for q in range(4)]
    factor_and_solve(
        load_columns,
        targets,
        lambda block: noise[pl.ds(8 * block, 8), :],
        cols,
        wide,
        inv_diag,
        halfway,
        out,
    )


def solver_scratch():
    return [
        pltpu.VMEM((RANK, 32, LANES), jnp.float32),
        pltpu.VMEM((RANK, RANK, LANES), jnp.float32),
        pltpu.VMEM((RANK, 8, LANES), jnp.float32),
        pltpu.VMEM((RANK, LANES), jnp.float32),
    ]


def pack_rows(rows):
    lead = rows.shape[:-2]
    split = rows.reshape(lead + (4, 2, 8, HALF))
    return jnp.swapaxes(split, -3, -2).reshape(lead + (32, LANES))


def solve_block(gram, right, pulled, prior_diag, prior_scale, noise, tau):
    share = right.shape[1]

    def fill(array, value=0.0):
        pad = [(0, 0)] * (array.ndim - 1) + [(0, HALF - share)]
        return jnp.pad(array, pad, constant_values=value)

    target = tau * right + prior_scale[:, None] * pulled
    prior = prior_scale[:, None] * fill(prior_diag, 1.0)[None, :]
    twice = lambda array: jnp.concatenate([array, array], axis=1)
    spec = pl.BlockSpec(memory_space=pltpu.VMEM)
    solved = pl.pallas_call(
        solve_kernel,
        out_shape=jax.ShapeDtypeStruct((RANK, LANES), jnp.float32),
        in_specs=[spec] * 4,
        out_specs=spec,
        scratch_shapes=solver_scratch(),
        compiler_params=pltpu.CompilerParams(vmem_limit_bytes=24 * 1024 * 1024),
        name="solve_sensors",
    )(tau * pack_rows(fill(gram)), pack_rows(fill(target)), twice(fill(noise)), twice(prior))
    return solved[:, :share]


def shifted(shard, axis, by):
    size = lax.axis_size(axis)
    pairs = [(i, i + by) for i in range(size) if 0 <= i + by < size]
    return lax.ppermute(shard, axis, pairs)


def general_shards(
    y_obs,
    observed,
    day_factor,
    slot_factor,
    sensor_factor,
    prior_scale,
    neighbours,
    edge_weight,
    noise,
):
    rank = sensor_factor.shape[0]
    block_len = sensor_factor.shape[1]
    all_slots = lax.all_gather(slot_factor, "day", axis=0, tiled=True)
    features = (day_factor[:, None, :] * all_slots[None, :, :]).reshape(-1, rank)
    row_total = features.shape[0] * lax.axis_size("day")
    outer_rows = (features[:, :, None] * features[:, None, :]).reshape(-1, rank * rank)
    mask_half = observed.astype(jnp.bfloat16)
    weighted = mask_half * y_obs
    dims = (((0,), (0,)), ((), ()))
    gram_sums = lax.dot_general(outer_rows, mask_half, dims, preferred_element_type=jnp.float32)
    right_sums = lax.dot_general(features, weighted, dims, preferred_element_type=jnp.float32)
    pieces = []
    for offset in (2, 1, 0, -1, -2):
        if offset == 0:
            pieces.append(sensor_factor)
        else:
            pieces.append(shifted(sensor_factor, "sensor", offset))
    window = jnp.concatenate(pieces, axis=1)
    base_col = (lax.axis_index("sensor") - 2) * block_len
    columns = neighbours - base_col
    picked = jnp.take(window, columns, axis=1).astype(jnp.float32)
    pulled = jnp.einsum("rns,ns->rs", picked, edge_weight)
    prior_diag = 1.0 + jnp.sum(edge_weight, axis=0)
    tau = 4.0 / row_total
    sums = jnp.concatenate([gram_sums, right_sums], axis=0)
    sums = lax.psum_scatter(sums, "day", scatter_dimension=1, tiled=True)
    share_len = sums.shape[1]
    first_col = lax.axis_index("day") * share_len
    part = lambda array: lax.dynamic_slice_in_dim(array, first_col, share_len, array.ndim - 1)
    solved = solve_block(
        sums[: rank * rank].reshape(rank, rank, share_len),
        sums[rank * rank :],
        part(pulled),
        part(prior_diag),
        prior_scale,
        part(noise),
        tau,
    )
    return lax.all_gather(solved, "day", axis=1, tiled=True)


COUNTS = [4 - block // 2 for block in range(BLOCKS)]
STARTS = [64 * sum(COUNTS[:block]) for block in range(BLOCKS)]
PACKED_ROWS = 64 * sum(COUNTS)
OFFSETS = (-2, -1, 1, 2)
DAY_ROWS = 16


def pack_pair(even, odd, own):
    low = lane_low(even.shape)
    if own:
        return jnp.where(low, even, pltpu.roll(odd, HALF, 1))
    return jnp.where(low, pltpu.roll(even, HALF, 1), odd)


def split_pairs(rows):
    count = rows.shape[0] // 16
    pairs = rows.reshape(count, 2, 8, LANES)
    return pairs[:, 0].reshape(8 * count, LANES), pairs[:, 1].reshape(8 * count, LANES)


def sweep_kernel(
    tau,
    days,
    y_hbm,
    observed_hbm,
    day_hbm,
    slot_hbm,
    factor_hbm,
    scale_hbm,
    neighbour_hbm,
    weight_hbm,
    noise_hbm,
    out_ref,
    day_ref,
    slot_ref,
    factor_ref,
    scale_ref,
    neighbour_ref,
    weight_ref,
    noise_ref,
    y_ref,
    observed_ref,
    mask_ref,
    weighted_ref,
    sent_mask,
    got_mask,
    sent_weighted,
    got_weighted,
    slot_wide,
    sent_factors,
    got_factors,
    window,
    features,
    wide_features,
    half_features,
    outer,
    gram,
    prior_ref,
    noise_own,
    packed_ref,
    peer_packed,
    found,
    cols,
    wide,
    inv_diag,
    halfway,
    load_sems,
    factor_sems,
    mask_sems,
    weighted_sems,
    window_send,
    window_recv,
    final_sems,
):
    day = lax.axis_index("day")
    sensor = lax.axis_index("sensor")
    sensors = lax.axis_size("sensor")
    rows = y_ref.shape[0]
    half_rows = rows // 2
    padded = mask_ref.shape[1]
    half_slots = slot_ref.shape[1]
    peer = {"day": 1 - day}
    mesh_id = pl.DeviceIdType.MESH
    f32, bf16 = jnp.float32, jnp.bfloat16

    barrier = pltpu.get_barrier_semaphore()
    pl.semaphore_signal(barrier, inc=1, device_id=peer, device_id_type=mesh_id)
    others = [lax.rem(sensor + sensors + offset, sensors) for offset in OFFSETS]
    for other in others:
        pl.semaphore_signal(barrier, inc=1, device_id={"sensor": other}, device_id_type=mesh_id)
    pairs = (
        (slot_hbm, slot_ref),
        (day_hbm, day_ref),
        (observed_hbm, observed_ref),
        (y_hbm, y_ref),
        (factor_hbm, factor_ref),
        (scale_hbm, scale_ref),
        (neighbour_hbm, neighbour_ref),
        (weight_hbm, weight_ref),
        (noise_hbm, noise_ref),
    )
    loads = []
    for index, (source, target) in enumerate(pairs):
        load = pltpu.make_async_copy(source, target, load_sems.at[index])
        load.start()
        loads.append(load)
    load_slots, load_days, load_mask, load_y, load_factor = loads[:5]

    def to_peer(source, target, sems):
        return pltpu.make_async_remote_copy(
            src_ref=source,
            dst_ref=target,
            send_sem=sems.at[0],
            recv_sem=sems.at[1],
            device_id=peer,
            device_id_type=mesh_id,
        )

    slot_wide[...] = jnp.zeros(slot_wide.shape, f32)
    load_slots.wait()
    slot_wide[pl.ds(0, RANK), pl.ds(0, half_slots)] = slot_ref[...].astype(f32)
    here = slot_wide[...].T[:half_slots]
    sent_factors[pl.ds(0, half_slots), :] = here.astype(bf16)
    load_days.wait()
    day_own = day_ref[...].astype(f32)
    day_own = jnp.concatenate([day_own, day_own], axis=1)
    tile_rows = lax.broadcasted_iota(jnp.int32, (DAY_ROWS, LANES), 0)
    day_tile = jnp.zeros((DAY_ROWS, LANES), f32)
    for index in range(days):
        day_tile = jnp.where(tile_rows == index, day_own[index : index + 1, :], day_tile)
    sent_factors[pl.ds(half_slots, DAY_ROWS), :] = day_tile.astype(bf16)

    def own_first(tile):
        return jnp.where(day == 0, tile, pltpu.roll(tile, HALF, 1))

    load_mask.wait()
    mask = own_first(observed_ref[...].astype(f32))
    mask_ref[0, pl.ds(0, rows), :] = mask.astype(bf16)
    sent_mask[...] = pack_pair(mask[:half_rows], mask[half_rows:], False).astype(bf16)

    load_factor.wait()
    pl.semaphore_wait(barrier, 1 + len(OFFSETS))
    factor_copy = to_peer(sent_factors, got_factors, factor_sems)
    factor_copy.start()
    mask_copy = to_peer(sent_mask, got_mask, mask_sems)
    mask_copy.start()
    window_copies = []
    for index, (offset, other) in enumerate(zip(OFFSETS, others)):
        copy = pltpu.make_async_remote_copy(
            src_ref=factor_ref,
            dst_ref=window.at[2 - offset],
            send_sem=window_send.at[index],
            recv_sem=window_recv.at[index],
            device_id={"sensor": other},
            device_id_type=mesh_id,
        )
        copy.start()
        window_copies.append(copy)

    load_y.wait()
    weighted = own_first(observed_ref[...].astype(f32) * y_ref[...].astype(f32))
    weighted_ref[0, pl.ds(0, rows), :] = weighted.astype(bf16)
    sent_weighted[...] = pack_pair(weighted[:half_rows], weighted[half_rows:], False).astype(bf16)
    weighted_copy = to_peer(sent_weighted, got_weighted, weighted_sems)
    weighted_copy.start()
    if padded > rows:
        empty = jnp.zeros((padded - rows, LANES), bf16)
        for part in range(2):
            mask_ref[part, pl.ds(rows, padded - rows), :] = empty
            weighted_ref[part, pl.ds(rows, padded - rows), :] = empty
        features[pl.ds(rows, padded - rows), :] = jnp.zeros((padded - rows, LANES), f32)

    factor_copy.wait()
    there = got_factors[pl.ds(0, half_slots), :].astype(f32)
    early = jnp.where(day == 0, here, there)
    late = jnp.where(day == 0, there, here)
    day_peer = got_factors[pl.ds(half_slots, DAY_ROWS), :].astype(f32)

    def make_features(part):
        day_rows = day_own if part == 0 else day_peer
        for index in range(days):
            row = day_rows[index : index + 1, :]
            at = index * 2 * half_slots
            features[pl.ds(at, half_slots), :] = early * row
            features[pl.ds(at + half_slots, half_slots), :] = late * row
        for index in range(padded // LANES):
            piece = features[pl.ds(index * LANES, LANES), :].T[:RANK]
            rounded = piece.astype(bf16)
            half_features[part, :, pl.ds(index * LANES, LANES)] = rounded
            wide_features[part, :, pl.ds(index * LANES, LANES)] = rounded.astype(f32)

    def gram_block(part, block):
        first = block // 2
        count = COUNTS[block]
        slab = outer.at[block % 2]
        for c in range(8):
            row = wide_features[part, pl.ds(8 * block + c, 1), :]
            row = jnp.broadcast_to(row, (16, padded)).astype(bf16)
            for q in range(first, 4):
                at = 16 * (c * count + q - first)
                slab[pl.ds(at, 16), :] = half_features[part, pl.ds(16 * q, 16), :] * row
        sums = jnp.dot(slab[pl.ds(0, 128 * count), :], mask_ref[part], preferred_element_type=f32)
        even, odd = split_pairs(sums)
        return pack_pair(even, odd, True)

    make_features(0)
    for block in range(BLOCKS):
        gram[pl.ds(STARTS[block], 64 * COUNTS[block]), :] = gram_block(0, block)
    make_features(1)

    for load in loads[5:]:
        load.wait()

    mine = (lax.broadcasted_iota(jnp.int32, (RANK, LANES), 1) >= HALF) == (day == 1)

    def spread_own(tile):
        return jnp.where(mine, tile, pltpu.roll(tile, HALF, 1))

    eye_rows = lax.broadcasted_iota(jnp.int32, (RANK, RANK), 0)
    eye_cols = lax.broadcasted_iota(jnp.int32, (RANK, RANK), 1)
    scale_row = jnp.broadcast_to(scale_ref[...], (RANK, RANK))
    scale = jnp.sum(jnp.where(eye_rows == eye_cols, scale_row, 0.0), axis=1, keepdims=True)
    scale = jnp.broadcast_to(scale, (RANK, LANES))
    prior_diag = 1.0 + jnp.sum(weight_ref[...], axis=0, keepdims=True)
    prior_ref[...] = scale * spread_own(jnp.broadcast_to(prior_diag, (RANK, LANES)))
    noise_own[...] = spread_own(noise_ref[...])

    base = (sensor - 2) * LANES
    column = neighbour_ref[...] - base
    weights = weight_ref[...]
    pulled = jnp.zeros((RANK, LANES), f32)
    for copy in window_copies:
        copy.wait()
    for slot in range(5):
        ids = lax.broadcasted_iota(jnp.int32, (LANES, LANES), 0) + slot * LANES
        picks = jnp.zeros((LANES, LANES), f32)
        for n in range(neighbour_ref.shape[0]):
            picks = picks + jnp.where(ids == column[n : n + 1, :], weights[n : n + 1, :], 0.0)
        high = picks.astype(bf16)
        low_part = (picks - high.astype(f32)).astype(bf16)
        source = factor_ref[...] if slot == 2 else window[slot]
        pulled = pulled + jnp.dot(source, high, preferred_element_type=f32)
        pulled = pulled + jnp.dot(source, low_part, preferred_element_type=f32)
    pulled = scale * spread_own(pulled)
    even, odd = split_pairs(pulled)
    pulled = jnp.where(lane_low(even.shape), even, odd)

    def unpack(packed, target):
        target[1, pl.ds(0, half_rows), :] = packed[...]
        turned = pltpu.roll(packed[...].astype(f32), HALF, 1)
        target[1, pl.ds(half_rows, half_rows), :] = turned.astype(bf16)

    mask_copy.wait()
    unpack(got_mask, mask_ref)
    for block in range(BLOCKS):
        at = pl.ds(STARTS[block], 64 * COUNTS[block])
        gram[at, :] = tau * (gram[at, :] + gram_block(1, block))

    weighted_copy.wait()
    unpack(got_weighted, weighted_ref)
    right = jnp.dot(half_features[0], weighted_ref[0], preferred_element_type=f32)
    right = right + jnp.dot(half_features[1], weighted_ref[1], preferred_element_type=f32)
    even, odd = split_pairs(right)
    target = tau * pack_pair(even, odd, True) + pulled

    def load_columns(block):
        first = block // 2
        count = COUNTS[block]
        prior = prior_ref[pl.ds(8 * block, 8), :]
        columns = []
        for c in range(8):
            tiles = []
            for q in range(first, 4):
                tiles.append(gram[pl.ds(STARTS[block] + 8 * (c * count + q - first), 8), :])
            tiles[0] = tiles[0] + diagonal_tile(block, c, prior)
            columns.append(tiles)
        return columns

    packed = factor_and_solve(
        load_columns,
        [target[8 * q : 8 * q + 8, :] for q in range(4)],
        lambda block: noise_own[pl.ds(8 * block, 8), :],
        cols,
        wide,
        inv_diag,
        halfway,
        found,
    )
    for q in range(4):
        packed_ref[pl.ds(8 * q, 8), :] = packed[q]
    final_copy = to_peer(packed_ref, peer_packed, final_sems)
    final_copy.start()
    final_copy.wait()
    mine_tile = (lax.broadcasted_iota(jnp.int32, (8, LANES), 1) >= HALF) == (day == 1)
    for tile in range(8):
        theirs = both_halves(peer_packed[pl.ds(8 * (tile // 2), 8), :], tile % 2 == 1)
        at = pl.ds(8 * tile, 8)
        out_ref[at, :] = jnp.where(mine_tile, found[at, :], theirs)


def paired_shards(
    y_obs,
    observed,
    day_factor,
    slot_factor,
    sensor_factor,
    prior_scale,
    neighbours,
    edge_weight,
    noise,
):
    rows = y_obs.shape[0]
    padded = -(-rows // 256) * 256
    half_slots = slot_factor.shape[0]
    slot_lanes = -(-half_slots // LANES) * LANES
    days = day_factor.shape[0]
    tau = 4.0 / (2 * rows)
    vmem = pl.BlockSpec(memory_space=pltpu.VMEM)
    hbm = pl.BlockSpec(memory_space=pl.ANY)
    f32, bf16 = jnp.float32, jnp.bfloat16
    dma = pltpu.SemaphoreType.DMA
    return pl.pallas_call(
        functools.partial(sweep_kernel, tau, days),
        out_shape=pltpu.VMEM((RANK, LANES), f32),
        in_specs=[hbm] * 9,
        out_specs=vmem,
        scratch_shapes=[
            pltpu.VMEM(day_factor.shape, bf16),
            pltpu.VMEM((RANK, half_slots), bf16),
            pltpu.VMEM((RANK, LANES), bf16),
            pltpu.VMEM((1, RANK), f32),
            pltpu.VMEM(neighbours.shape, jnp.int32),
            pltpu.VMEM(edge_weight.shape, f32),
            pltpu.VMEM((RANK, LANES), f32),
            pltpu.VMEM((rows, LANES), bf16),
            pltpu.VMEM((rows, LANES), jnp.int32),
            pltpu.VMEM((2, padded, LANES), bf16),
            pltpu.VMEM((2, padded, LANES), bf16),
            pltpu.VMEM((rows // 2, LANES), bf16),
            pltpu.VMEM((rows // 2, LANES), bf16),
            pltpu.VMEM((rows // 2, LANES), bf16),
            pltpu.VMEM((rows // 2, LANES), bf16),
            pltpu.VMEM((LANES, slot_lanes), f32),
            pltpu.VMEM((half_slots + DAY_ROWS, LANES), bf16),
            pltpu.VMEM((half_slots + DAY_ROWS, LANES), bf16),
            pltpu.VMEM((5, RANK, LANES), bf16),
            pltpu.VMEM((padded, LANES), f32),
            pltpu.VMEM((2, RANK, padded), f32),
            pltpu.VMEM((2, RANK, padded), bf16),
            pltpu.VMEM((2, 512, padded), bf16),
            pltpu.VMEM((PACKED_ROWS, LANES), f32),
            pltpu.VMEM((RANK, LANES), f32),
            pltpu.VMEM((RANK, LANES), f32),
            pltpu.VMEM((32, LANES), f32),
            pltpu.VMEM((32, LANES), f32),
            pltpu.VMEM((RANK, LANES), f32),
        ]
        + solver_scratch()
        + [dma((9,)), dma((2,)), dma((2,)), dma((2,)), dma((4,)), dma((4,)), dma((2,))],
        compiler_params=pltpu.CompilerParams(
            collective_id=0, has_side_effects=True, vmem_limit_bytes=VMEM_BYTES
        ),
        name="sweep_sensors",
    )(
        y_obs,
        observed,
        day_factor,
        slot_factor.T,
        sensor_factor,
        prior_scale.reshape(1, RANK),
        neighbours,
        edge_weight,
        noise,
    )


def solution(mesh):
    sizes = dict(mesh.shape)

    def shards(*arrays):
        y_obs, slot_factor = arrays[0], arrays[3]
        fits = sizes["day"] == 2 and sizes["sensor"] >= 5 and y_obs.shape[1] == LANES
        fits = fits and y_obs.shape[0] % 32 == 0 and slot_factor.shape[0] % 16 == 0
        fits = fits and arrays[2].shape[0] <= DAY_ROWS
        return paired_shards(*arrays) if fits else general_shards(*arrays)

    return jax.shard_map(
        shards,
        mesh=mesh,
        in_specs=(
            P("day", "sensor"),
            P("day", "sensor"),
            P("day", None),
            P("day", None),
            P(None, "sensor"),
            P(),
            P(None, "sensor"),
            P(None, "sensor"),
            P(None, "sensor"),
        ),
        out_specs=P(None, "sensor"),
        check_vma=False,
    )
```

```python
import functools

import jax
import jax.numpy as jnp
from jax import lax
from jax.experimental import pallas as pl
from jax.experimental.pallas import tpu as pltpu
from jax.sharding import PartitionSpec as P

RANK = 64
LANES = 128
HALF = 64
BLOCKS = RANK // 8
VMEM_BYTES = 60 * 1024 * 1024


def lane_low(shape):
    return lax.broadcasted_iota(jnp.int32, shape, len(shape) - 1) < HALF


def both_halves(tile, upper):
    other = pltpu.roll(tile, HALF, 1)
    low = lane_low(tile.shape)
    return jnp.where(low, other, tile) if upper else jnp.where(low, tile, other)


def row_of(tile, index):
    return jnp.broadcast_to(tile[index : index + 1, :], tile.shape)


def factor_and_solve(load_columns, target, noise_tile, cols, wide, inv_diag, halfway, found):
    target = list(target)
    for block in range(BLOCKS):
        first = block // 2
        upper = block % 2 == 1
        count = 4 - first
        columns = load_columns(block)
        if block > 0:

            def subtract(k, carry):
                done = [cols[k, pl.ds(8 * q, 8), :] for q in range(first, 4)]
                out = []
                for c in range(8):
                    scale = jnp.broadcast_to(wide[k, pl.ds(8 * block + c, 1), :], (8, LANES))
                    out.extend(carry[c * count + q] - done[q] * scale for q in range(count))
                return tuple(out)

            flat = tuple(tile for column in columns for tile in column)
            flat = lax.fori_loop(0, 8 * block, subtract, flat, unroll=2)
            columns = [list(flat[c * count : (c + 1) * count]) for c in range(8)]
        corner = [both_halves(column[0], upper) for column in columns]
        side = both_halves(target[first], upper)
        for c in range(8):
            j = 8 * block + c
            inverse = lax.rsqrt(row_of(corner[c], c))
            corner[c] = corner[c] * inverse
            columns[c] = [tile * inverse for tile in columns[c]]
            solved = row_of(side, c) * inverse
            side = side - corner[c] * solved
            for q in range(count):
                target[first + q] = target[first + q] - columns[c][q] * solved
            for later in range(c + 1, 8):
                scale = row_of(corner[c], later)
                corner[later] = corner[later] - corner[c] * scale
                columns[later] = [
                    tile - own * scale for tile, own in zip(columns[later], columns[c])
                ]
            inv_diag[j] = inverse
            halfway[pl.ds(j, 1), :] = solved[0:1, :]
        for c in range(8):
            j = 8 * block + c
            for q in range(count):
                tile = columns[c][q]
                row = 16 * (first + q)
                cols[j, pl.ds(8 * (first + q), 8), :] = tile
                if row >= 8 * block:
                    wide[j, pl.ds(row, 8), :] = both_halves(tile, False)
                wide[j, pl.ds(row + 8, 8), :] = both_halves(tile, True)

    packed = [None] * 4
    low = lane_low((8, LANES))
    below = None
    for block in reversed(range(BLOCKS)):
        first = block // 2
        upper = block % 2 == 1
        right = halfway[pl.ds(8 * block, 8), :] + noise_tile(block)
        remain = []
        for c in range(8):
            j = 8 * block + c
            total = row_of(right, c)
            parts = None
            for q in range(first, 4):
                if q == first and upper:
                    continue
                if q == first:
                    term = jnp.where(low, 0.0, cols[j, pl.ds(8 * q, 8), :] * below)
                else:
                    term = cols[j, pl.ds(8 * q, 8), :] * packed[q]
                parts = term if parts is None else parts + term
            if parts is not None:
                sums = jnp.sum(parts, axis=0, keepdims=True)
                sums = jnp.broadcast_to(sums, (8, LANES))
                total = total - (sums + pltpu.roll(sums, HALF, 1))
            remain.append(total)
        values = [None] * 8
        for c in reversed(range(8)):
            values[c] = remain[c] * inv_diag[8 * block + c]
            for earlier in range(c):
                scale = jnp.broadcast_to(
                    wide[8 * block + earlier, pl.ds(8 * block + c, 1), :], (8, LANES)
                )
                remain[earlier] = remain[earlier] - scale * values[c]
        rows = lax.broadcasted_iota(jnp.int32, (8, LANES), 0)
        tile = values[0]
        for c in range(1, 8):
            tile = jnp.where(rows == c, values[c], tile)
        found[pl.ds(8 * block, 8), :] = tile
        if upper:
            below = tile
        else:
            packed[first] = jnp.where(low, tile, below)
            below = None
    return packed


def diagonal_tile(block, c, value):
    shape = (8, LANES)
    rows = lax.broadcasted_iota(jnp.int32, shape, 0)
    low = lane_low(shape)
    half = low if block % 2 == 0 else jnp.logical_not(low)
    return jnp.where((rows == c) & half, value, 0.0)


def solve_kernel(squares, target, noise, prior, out, cols, wide, inv_diag, halfway):
    def load_columns(block):
        first = block // 2
        own = prior[pl.ds(8 * block, 8), :]
        columns = []
        for c in range(8):
            j = 8 * block + c
            tiles = [squares[j, pl.ds(8 * q, 8), :] for q in range(first, 4)]
            tiles[0] = tiles[0] + diagonal_tile(block, c, own)
            columns.append(tiles)
        return columns

    targets = [target[pl.ds(8 * q, 8), :] for q in range(4)]
    factor_and_solve(
        load_columns,
        targets,
        lambda block: noise[pl.ds(8 * block, 8), :],
        cols,
        wide,
        inv_diag,
        halfway,
        out,
    )


def solver_scratch():
    return [
        pltpu.VMEM((RANK, 32, LANES), jnp.float32),
        pltpu.VMEM((RANK, RANK, LANES), jnp.float32),
        pltpu.VMEM((RANK, 8, LANES), jnp.float32),
        pltpu.VMEM((RANK, LANES), jnp.float32),
    ]


def pack_rows(rows):
    lead = rows.shape[:-2]
    split = rows.reshape(lead + (4, 2, 8, HALF))
    return jnp.swapaxes(split, -3, -2).reshape(lead + (32, LANES))


def solve_block(gram, right, pulled, prior_diag, prior_scale, noise, tau):
    share = right.shape[1]

    def fill(array, value=0.0):
        pad = [(0, 0)] * (array.ndim - 1) + [(0, HALF - share)]
        return jnp.pad(array, pad, constant_values=value)

    target = tau * right + prior_scale[:, None] * pulled
    prior = prior_scale[:, None] * fill(prior_diag, 1.0)[None, :]
    twice = lambda array: jnp.concatenate([array, array], axis=1)
    spec = pl.BlockSpec(memory_space=pltpu.VMEM)
    solved = pl.pallas_call(
        solve_kernel,
        out_shape=jax.ShapeDtypeStruct((RANK, LANES), jnp.float32),
        in_specs=[spec] * 4,
        out_specs=spec,
        scratch_shapes=solver_scratch(),
        compiler_params=pltpu.CompilerParams(vmem_limit_bytes=24 * 1024 * 1024),
        name="solve_sensors",
    )(tau * pack_rows(fill(gram)), pack_rows(fill(target)), twice(fill(noise)), twice(prior))
    return solved[:, :share]


def shifted(shard, axis, by):
    size = lax.axis_size(axis)
    pairs = [(i, i + by) for i in range(size) if 0 <= i + by < size]
    return lax.ppermute(shard, axis, pairs)


def general_shards(
    y_obs,
    observed,
    day_factor,
    slot_factor,
    sensor_factor,
    prior_scale,
    neighbours,
    edge_weight,
    noise,
):
    rank = sensor_factor.shape[0]
    block_len = sensor_factor.shape[1]
    all_slots = lax.all_gather(slot_factor, "day", axis=0, tiled=True)
    features = (day_factor[:, None, :] * all_slots[None, :, :]).reshape(-1, rank)
    row_total = features.shape[0] * lax.axis_size("day")
    outer_rows = (features[:, :, None] * features[:, None, :]).reshape(-1, rank * rank)
    mask_half = observed.astype(jnp.bfloat16)
    weighted = mask_half * y_obs
    dims = (((0,), (0,)), ((), ()))
    gram_sums = lax.dot_general(outer_rows, mask_half, dims, preferred_element_type=jnp.float32)
    right_sums = lax.dot_general(features, weighted, dims, preferred_element_type=jnp.float32)
    pieces = []
    for offset in (2, 1, 0, -1, -2):
        if offset == 0:
            pieces.append(sensor_factor)
        else:
            pieces.append(shifted(sensor_factor, "sensor", offset))
    window = jnp.concatenate(pieces, axis=1)
    base_col = (lax.axis_index("sensor") - 2) * block_len
    columns = neighbours - base_col
    picked = jnp.take(window, columns, axis=1).astype(jnp.float32)
    pulled = jnp.einsum("rns,ns->rs", picked, edge_weight)
    prior_diag = 1.0 + jnp.sum(edge_weight, axis=0)
    tau = 4.0 / row_total
    sums = jnp.concatenate([gram_sums, right_sums], axis=0)
    sums = lax.psum_scatter(sums, "day", scatter_dimension=1, tiled=True)
    share_len = sums.shape[1]
    first_col = lax.axis_index("day") * share_len
    part = lambda array: lax.dynamic_slice_in_dim(array, first_col, share_len, array.ndim - 1)
    solved = solve_block(
        sums[: rank * rank].reshape(rank, rank, share_len),
        sums[rank * rank :],
        part(pulled),
        part(prior_diag),
        prior_scale,
        part(noise),
        tau,
    )
    return lax.all_gather(solved, "day", axis=1, tiled=True)


COUNTS = [4 - block // 2 for block in range(BLOCKS)]
STARTS = [64 * sum(COUNTS[:block]) for block in range(BLOCKS)]
PACKED_ROWS = 64 * sum(COUNTS)
OFFSETS = (-2, -1, 1, 2)
DAY_ROWS = 16


def pack_pair(even, odd, own):
    low = lane_low(even.shape)
    if own:
        return jnp.where(low, even, pltpu.roll(odd, HALF, 1))
    return jnp.where(low, pltpu.roll(even, HALF, 1), odd)


def split_pairs(rows):
    count = rows.shape[0] // 16
    pairs = rows.reshape(count, 2, 8, LANES)
    return pairs[:, 0].reshape(8 * count, LANES), pairs[:, 1].reshape(8 * count, LANES)


def sweep_kernel(
    tau,
    days,
    y_hbm,
    observed_hbm,
    day_hbm,
    slot_hbm,
    factor_hbm,
    scale_hbm,
    neighbour_hbm,
    weight_hbm,
    noise_hbm,
    out_ref,
    day_ref,
    slot_ref,
    factor_ref,
    scale_ref,
    neighbour_ref,
    weight_ref,
    noise_ref,
    y_ref,
    observed_ref,
    mask_ref,
    weighted_ref,
    sent_mask,
    got_mask,
    own_right,
    sent_right,
    got_right,
    slot_wide,
    sent_factors,
    got_factors,
    window,
    features,
    wide_features,
    half_features,
    outer,
    gram,
    prior_ref,
    noise_own,
    packed_ref,
    peer_packed,
    found,
    cols,
    wide,
    inv_diag,
    halfway,
    load_sems,
    factor_sems,
    mask_sems,
    right_sems,
    window_send,
    window_recv,
    final_sems,
):
    day = lax.axis_index("day")
    sensor = lax.axis_index("sensor")
    sensors = lax.axis_size("sensor")
    rows = y_ref.shape[0]
    half_rows = rows // 2
    padded = mask_ref.shape[1]
    half_slots = slot_ref.shape[1]
    peer = {"day": 1 - day}
    mesh_id = pl.DeviceIdType.MESH
    f32, bf16 = jnp.float32, jnp.bfloat16

    barrier = pltpu.get_barrier_semaphore()
    pl.semaphore_signal(barrier, inc=1, device_id=peer, device_id_type=mesh_id)
    others = [lax.rem(sensor + sensors + offset, sensors) for offset in OFFSETS]
    for other in others:
        pl.semaphore_signal(barrier, inc=1, device_id={"sensor": other}, device_id_type=mesh_id)
    pairs = (
        (slot_hbm, slot_ref),
        (day_hbm, day_ref),
        (observed_hbm, observed_ref),
        (y_hbm, y_ref),
        (factor_hbm, factor_ref),
        (scale_hbm, scale_ref),
        (neighbour_hbm, neighbour_ref),
        (weight_hbm, weight_ref),
        (noise_hbm, noise_ref),
    )
    loads = []
    for index, (source, target) in enumerate(pairs):
        load = pltpu.make_async_copy(source, target, load_sems.at[index])
        load.start()
        loads.append(load)
    load_slots, load_days, load_mask, load_y, load_factor = loads[:5]

    def to_peer(source, target, sems):
        return pltpu.make_async_remote_copy(
            src_ref=source,
            dst_ref=target,
            send_sem=sems.at[0],
            recv_sem=sems.at[1],
            device_id=peer,
            device_id_type=mesh_id,
        )

    slot_wide[...] = jnp.zeros(slot_wide.shape, f32)
    load_slots.wait()
    slot_wide[pl.ds(0, RANK), pl.ds(0, half_slots)] = slot_ref[...].astype(f32)
    here = slot_wide[...].T[:half_slots]
    sent_factors[pl.ds(0, half_slots), :] = here.astype(bf16)
    load_days.wait()
    day_own = day_ref[...].astype(f32)
    day_own = jnp.concatenate([day_own, day_own], axis=1)
    tile_rows = lax.broadcasted_iota(jnp.int32, (DAY_ROWS, LANES), 0)
    day_tile = jnp.zeros((DAY_ROWS, LANES), f32)
    for index in range(days):
        day_tile = jnp.where(tile_rows == index, day_own[index : index + 1, :], day_tile)
    sent_factors[pl.ds(half_slots, DAY_ROWS), :] = day_tile.astype(bf16)

    def own_first(tile):
        return jnp.where(day == 0, tile, pltpu.roll(tile, HALF, 1))

    load_mask.wait()
    mask = own_first(observed_ref[...].astype(f32))
    mask_ref[0, pl.ds(0, rows), :] = mask.astype(bf16)
    sent_mask[...] = pack_pair(mask[:half_rows], mask[half_rows:], False).astype(bf16)

    load_factor.wait()
    pl.semaphore_wait(barrier, 1 + len(OFFSETS))
    factor_copy = to_peer(sent_factors, got_factors, factor_sems)
    factor_copy.start()
    mask_copy = to_peer(sent_mask, got_mask, mask_sems)
    mask_copy.start()
    window_copies = []
    for index, (offset, other) in enumerate(zip(OFFSETS, others)):
        copy = pltpu.make_async_remote_copy(
            src_ref=factor_ref,
            dst_ref=window.at[2 - offset],
            send_sem=window_send.at[index],
            recv_sem=window_recv.at[index],
            device_id={"sensor": other},
            device_id_type=mesh_id,
        )
        copy.start()
        window_copies.append(copy)

    load_y.wait()
    weighted = own_first(observed_ref[...].astype(f32) * y_ref[...].astype(f32))
    weighted_ref[pl.ds(0, rows), :] = weighted.astype(bf16)
    if padded > rows:
        empty = jnp.zeros((padded - rows, LANES), bf16)
        for part in range(2):
            mask_ref[part, pl.ds(rows, padded - rows), :] = empty
        weighted_ref[pl.ds(rows, padded - rows), :] = empty
        features[pl.ds(rows, padded - rows), :] = jnp.zeros((padded - rows, LANES), f32)

    factor_copy.wait()
    there = got_factors[pl.ds(0, half_slots), :].astype(f32)
    early = jnp.where(day == 0, here, there)
    late = jnp.where(day == 0, there, here)
    day_peer = got_factors[pl.ds(half_slots, DAY_ROWS), :].astype(f32)

    def make_features(part):
        day_rows = day_own if part == 0 else day_peer
        for index in range(days):
            row = day_rows[index : index + 1, :]
            at = index * 2 * half_slots
            features[pl.ds(at, half_slots), :] = early * row
            features[pl.ds(at + half_slots, half_slots), :] = late * row
        for index in range(padded // LANES):
            piece = features[pl.ds(index * LANES, LANES), :].T[:RANK]
            rounded = piece.astype(bf16)
            half_features[part, :, pl.ds(index * LANES, LANES)] = rounded
            wide_features[part, :, pl.ds(index * LANES, LANES)] = rounded.astype(f32)

    def gram_block(part, block):
        first = block // 2
        count = COUNTS[block]
        slab = outer.at[block % 2]
        for c in range(8):
            row = wide_features[part, pl.ds(8 * block + c, 1), :]
            row = jnp.broadcast_to(row, (16, padded)).astype(bf16)
            for q in range(first, 4):
                at = 16 * (c * count + q - first)
                slab[pl.ds(at, 16), :] = half_features[part, pl.ds(16 * q, 16), :] * row
        sums = jnp.dot(slab[pl.ds(0, 128 * count), :], mask_ref[part], preferred_element_type=f32)
        even, odd = split_pairs(sums)
        return pack_pair(even, odd, True)

    make_features(0)
    right = jnp.dot(half_features[0], weighted_ref[...], preferred_element_type=f32)
    even, odd = split_pairs(right)
    own_right[...] = pack_pair(even, odd, True)
    sent_right[...] = pack_pair(even, odd, False)
    right_copy = to_peer(sent_right, got_right, right_sems)
    right_copy.start()
    for block in range(BLOCKS):
        gram[pl.ds(STARTS[block], 64 * COUNTS[block]), :] = gram_block(0, block)
    make_features(1)

    for load in loads[5:]:
        load.wait()

    mine = (lax.broadcasted_iota(jnp.int32, (RANK, LANES), 1) >= HALF) == (day == 1)

    def spread_own(tile):
        return jnp.where(mine, tile, pltpu.roll(tile, HALF, 1))

    eye_rows = lax.broadcasted_iota(jnp.int32, (RANK, RANK), 0)
    eye_cols = lax.broadcasted_iota(jnp.int32, (RANK, RANK), 1)
    scale_row = jnp.broadcast_to(scale_ref[...], (RANK, RANK))
    scale = jnp.sum(jnp.where(eye_rows == eye_cols, scale_row, 0.0), axis=1, keepdims=True)
    scale = jnp.broadcast_to(scale, (RANK, LANES))
    prior_diag = 1.0 + jnp.sum(weight_ref[...], axis=0, keepdims=True)
    prior_ref[...] = scale * spread_own(jnp.broadcast_to(prior_diag, (RANK, LANES)))
    noise_own[...] = spread_own(noise_ref[...])

    base = (sensor - 2) * LANES
    column = neighbour_ref[...] - base
    weights = weight_ref[...]
    pulled = jnp.zeros((RANK, LANES), f32)
    for copy in window_copies:
        copy.wait()
    for slot in range(5):
        ids = lax.broadcasted_iota(jnp.int32, (LANES, LANES), 0) + slot * LANES
        picks = jnp.zeros((LANES, LANES), f32)
        for n in range(neighbour_ref.shape[0]):
            picks = picks + jnp.where(ids == column[n : n + 1, :], weights[n : n + 1, :], 0.0)
        high = picks.astype(bf16)
        low_part = (picks - high.astype(f32)).astype(bf16)
        source = factor_ref[...] if slot == 2 else window[slot]
        pulled = pulled + jnp.dot(source, high, preferred_element_type=f32)
        pulled = pulled + jnp.dot(source, low_part, preferred_element_type=f32)
    pulled = scale * spread_own(pulled)
    even, odd = split_pairs(pulled)
    pulled = jnp.where(lane_low(even.shape), even, odd)

    mask_copy.wait()
    mask_ref[1, pl.ds(0, half_rows), :] = got_mask[...]
    turned = pltpu.roll(got_mask[...].astype(f32), HALF, 1)
    mask_ref[1, pl.ds(half_rows, half_rows), :] = turned.astype(bf16)
    for block in range(BLOCKS):
        at = pl.ds(STARTS[block], 64 * COUNTS[block])
        gram[at, :] = tau * (gram[at, :] + gram_block(1, block))

    right_copy.wait()
    target = tau * (own_right[...] + got_right[...]) + pulled

    def load_columns(block):
        first = block // 2
        count = COUNTS[block]
        prior = prior_ref[pl.ds(8 * block, 8), :]
        columns = []
        for c in range(8):
            tiles = []
            for q in range(first, 4):
                tiles.append(gram[pl.ds(STARTS[block] + 8 * (c * count + q - first), 8), :])
            tiles[0] = tiles[0] + diagonal_tile(block, c, prior)
            columns.append(tiles)
        return columns

    packed = factor_and_solve(
        load_columns,
        [target[8 * q : 8 * q + 8, :] for q in range(4)],
        lambda block: noise_own[pl.ds(8 * block, 8), :],
        cols,
        wide,
        inv_diag,
        halfway,
        found,
    )
    for q in range(4):
        packed_ref[pl.ds(8 * q, 8), :] = packed[q]
    final_copy = to_peer(packed_ref, peer_packed, final_sems)
    final_copy.start()
    final_copy.wait()
    mine_tile = (lax.broadcasted_iota(jnp.int32, (8, LANES), 1) >= HALF) == (day == 1)
    for tile in range(8):
        theirs = both_halves(peer_packed[pl.ds(8 * (tile // 2), 8), :], tile % 2 == 1)
        at = pl.ds(8 * tile, 8)
        out_ref[at, :] = jnp.where(mine_tile, found[at, :], theirs)


def paired_shards(
    y_obs,
    observed,
    day_factor,
    slot_factor,
    sensor_factor,
    prior_scale,
    neighbours,
    edge_weight,
    noise,
):
    rows = y_obs.shape[0]
    padded = -(-rows // 256) * 256
    half_slots = slot_factor.shape[0]
    slot_lanes = -(-half_slots // LANES) * LANES
    days = day_factor.shape[0]
    tau = 4.0 / (2 * rows)
    vmem = pl.BlockSpec(memory_space=pltpu.VMEM)
    hbm = pl.BlockSpec(memory_space=pl.ANY)
    f32, bf16 = jnp.float32, jnp.bfloat16
    dma = pltpu.SemaphoreType.DMA
    return pl.pallas_call(
        functools.partial(sweep_kernel, tau, days),
        out_shape=pltpu.VMEM((RANK, LANES), f32),
        in_specs=[hbm] * 9,
        out_specs=vmem,
        scratch_shapes=[
            pltpu.VMEM(day_factor.shape, bf16),
            pltpu.VMEM((RANK, half_slots), bf16),
            pltpu.VMEM((RANK, LANES), bf16),
            pltpu.VMEM((1, RANK), f32),
            pltpu.VMEM(neighbours.shape, jnp.int32),
            pltpu.VMEM(edge_weight.shape, f32),
            pltpu.VMEM((RANK, LANES), f32),
            pltpu.VMEM((rows, LANES), bf16),
            pltpu.VMEM((rows, LANES), jnp.int32),
            pltpu.VMEM((2, padded, LANES), bf16),
            pltpu.VMEM((padded, LANES), bf16),
            pltpu.VMEM((rows // 2, LANES), bf16),
            pltpu.VMEM((rows // 2, LANES), bf16),
            pltpu.VMEM((32, LANES), f32),
            pltpu.VMEM((32, LANES), f32),
            pltpu.VMEM((32, LANES), f32),
            pltpu.VMEM((LANES, slot_lanes), f32),
            pltpu.VMEM((half_slots + DAY_ROWS, LANES), bf16),
            pltpu.VMEM((half_slots + DAY_ROWS, LANES), bf16),
            pltpu.VMEM((5, RANK, LANES), bf16),
            pltpu.VMEM((padded, LANES), f32),
            pltpu.VMEM((2, RANK, padded), f32),
            pltpu.VMEM((2, RANK, padded), bf16),
            pltpu.VMEM((2, 512, padded), bf16),
            pltpu.VMEM((PACKED_ROWS, LANES), f32),
            pltpu.VMEM((RANK, LANES), f32),
            pltpu.VMEM((RANK, LANES), f32),
            pltpu.VMEM((32, LANES), f32),
            pltpu.VMEM((32, LANES), f32),
            pltpu.VMEM((RANK, LANES), f32),
        ]
        + solver_scratch()
        + [dma((9,)), dma((2,)), dma((2,)), dma((2,)), dma((4,)), dma((4,)), dma((2,))],
        compiler_params=pltpu.CompilerParams(
            collective_id=0, has_side_effects=True, vmem_limit_bytes=VMEM_BYTES
        ),
        name="sweep_sensors",
    )(
        y_obs,
        observed,
        day_factor,
        slot_factor.T,
        sensor_factor,
        prior_scale.reshape(1, RANK),
        neighbours,
        edge_weight,
        noise,
    )


def solution(mesh):
    sizes = dict(mesh.shape)

    def shards(*arrays):
        y_obs, slot_factor = arrays[0], arrays[3]
        fits = sizes["day"] == 2 and sizes["sensor"] >= 5 and y_obs.shape[1] == LANES
        fits = fits and y_obs.shape[0] % 32 == 0 and slot_factor.shape[0] % 16 == 0
        fits = fits and arrays[2].shape[0] <= DAY_ROWS
        return paired_shards(*arrays) if fits else general_shards(*arrays)

    return jax.shard_map(
        shards,
        mesh=mesh,
        in_specs=(
            P("day", "sensor"),
            P("day", "sensor"),
            P("day", None),
            P("day", None),
            P(None, "sensor"),
            P(),
            P(None, "sensor"),
            P(None, "sensor"),
            P(None, "sensor"),
        ),
        out_specs=P(None, "sensor"),
        check_vma=False,
    )
```

```python
import functools

import jax
import jax.numpy as jnp
from jax import lax
from jax.experimental import pallas as pl
from jax.experimental.pallas import tpu as pltpu
from jax.sharding import PartitionSpec as P

RANK = 64
LANES = 128
HALF = 64
BLOCKS = RANK // 8
VMEM_BYTES = 60 * 1024 * 1024


def lane_low(shape):
    return lax.broadcasted_iota(jnp.int32, shape, len(shape) - 1) < HALF


def both_halves(tile, upper):
    other = pltpu.roll(tile, HALF, 1)
    low = lane_low(tile.shape)
    return jnp.where(low, other, tile) if upper else jnp.where(low, tile, other)


def row_of(tile, index):
    return jnp.broadcast_to(tile[index : index + 1, :], tile.shape)


def factor_and_solve(load_columns, target, noise_tile, cols, wide, inv_diag, halfway, found):
    target = list(target)
    for block in range(BLOCKS):
        first = block // 2
        upper = block % 2 == 1
        count = 4 - first
        columns = load_columns(block)
        if block > 0:

            def subtract(k, carry):
                done = [cols[k, pl.ds(8 * q, 8), :] for q in range(first, 4)]
                out = []
                for c in range(8):
                    scale = jnp.broadcast_to(wide[k, pl.ds(8 * block + c, 1), :], (8, LANES))
                    out.extend(carry[c * count + q] - done[q] * scale for q in range(count))
                return tuple(out)

            flat = tuple(tile for column in columns for tile in column)
            flat = lax.fori_loop(0, 8 * block, subtract, flat, unroll=2)
            columns = [list(flat[c * count : (c + 1) * count]) for c in range(8)]
        corner = [both_halves(column[0], upper) for column in columns]
        side = both_halves(target[first], upper)
        for c in range(8):
            j = 8 * block + c
            inverse = lax.rsqrt(row_of(corner[c], c))
            corner[c] = corner[c] * inverse
            columns[c] = [tile * inverse for tile in columns[c]]
            solved = row_of(side, c) * inverse
            side = side - corner[c] * solved
            for q in range(count):
                target[first + q] = target[first + q] - columns[c][q] * solved
            for later in range(c + 1, 8):
                scale = row_of(corner[c], later)
                corner[later] = corner[later] - corner[c] * scale
                columns[later] = [
                    tile - own * scale for tile, own in zip(columns[later], columns[c])
                ]
            inv_diag[j] = inverse
            halfway[pl.ds(j, 1), :] = solved[0:1, :]
        for c in range(8):
            j = 8 * block + c
            for q in range(count):
                tile = columns[c][q]
                row = 16 * (first + q)
                cols[j, pl.ds(8 * (first + q), 8), :] = tile
                if row >= 8 * block:
                    wide[j, pl.ds(row, 8), :] = both_halves(tile, False)
                wide[j, pl.ds(row + 8, 8), :] = both_halves(tile, True)

    packed = [None] * 4
    low = lane_low((8, LANES))
    below = None
    for block in reversed(range(BLOCKS)):
        first = block // 2
        upper = block % 2 == 1
        right = halfway[pl.ds(8 * block, 8), :] + noise_tile(block)
        remain = []
        for c in range(8):
            j = 8 * block + c
            total = row_of(right, c)
            parts = None
            for q in range(first, 4):
                if q == first and upper:
                    continue
                if q == first:
                    term = jnp.where(low, 0.0, cols[j, pl.ds(8 * q, 8), :] * below)
                else:
                    term = cols[j, pl.ds(8 * q, 8), :] * packed[q]
                parts = term if parts is None else parts + term
            if parts is not None:
                sums = jnp.sum(parts, axis=0, keepdims=True)
                sums = jnp.broadcast_to(sums, (8, LANES))
                total = total - (sums + pltpu.roll(sums, HALF, 1))
            remain.append(total)
        values = [None] * 8
        for c in reversed(range(8)):
            values[c] = remain[c] * inv_diag[8 * block + c]
            for earlier in range(c):
                scale = jnp.broadcast_to(
                    wide[8 * block + earlier, pl.ds(8 * block + c, 1), :], (8, LANES)
                )
                remain[earlier] = remain[earlier] - scale * values[c]
        rows = lax.broadcasted_iota(jnp.int32, (8, LANES), 0)
        tile = values[0]
        for c in range(1, 8):
            tile = jnp.where(rows == c, values[c], tile)
        found[pl.ds(8 * block, 8), :] = tile
        if upper:
            below = tile
        else:
            packed[first] = jnp.where(low, tile, below)
            below = None
    return packed


def diagonal_tile(block, c, value):
    shape = (8, LANES)
    rows = lax.broadcasted_iota(jnp.int32, shape, 0)
    low = lane_low(shape)
    half = low if block % 2 == 0 else jnp.logical_not(low)
    return jnp.where((rows == c) & half, value, 0.0)


def solve_kernel(squares, target, noise, prior, out, cols, wide, inv_diag, halfway):
    def load_columns(block):
        first = block // 2
        own = prior[pl.ds(8 * block, 8), :]
        columns = []
        for c in range(8):
            j = 8 * block + c
            tiles = [squares[j, pl.ds(8 * q, 8), :] for q in range(first, 4)]
            tiles[0] = tiles[0] + diagonal_tile(block, c, own)
            columns.append(tiles)
        return columns

    targets = [target[pl.ds(8 * q, 8), :] for q in range(4)]
    factor_and_solve(
        load_columns,
        targets,
        lambda block: noise[pl.ds(8 * block, 8), :],
        cols,
        wide,
        inv_diag,
        halfway,
        out,
    )


def solver_scratch():
    return [
        pltpu.VMEM((RANK, 32, LANES), jnp.float32),
        pltpu.VMEM((RANK, RANK, LANES), jnp.float32),
        pltpu.VMEM((RANK, 8, LANES), jnp.float32),
        pltpu.VMEM((RANK, LANES), jnp.float32),
    ]


def pack_rows(rows):
    lead = rows.shape[:-2]
    split = rows.reshape(lead + (4, 2, 8, HALF))
    return jnp.swapaxes(split, -3, -2).reshape(lead + (32, LANES))


def solve_block(gram, right, pulled, prior_diag, prior_scale, noise, tau):
    share = right.shape[1]

    def fill(array, value=0.0):
        pad = [(0, 0)] * (array.ndim - 1) + [(0, HALF - share)]
        return jnp.pad(array, pad, constant_values=value)

    target = tau * right + prior_scale[:, None] * pulled
    prior = prior_scale[:, None] * fill(prior_diag, 1.0)[None, :]
    twice = lambda array: jnp.concatenate([array, array], axis=1)
    spec = pl.BlockSpec(memory_space=pltpu.VMEM)
    solved = pl.pallas_call(
        solve_kernel,
        out_shape=jax.ShapeDtypeStruct((RANK, LANES), jnp.float32),
        in_specs=[spec] * 4,
        out_specs=spec,
        scratch_shapes=solver_scratch(),
        compiler_params=pltpu.CompilerParams(vmem_limit_bytes=24 * 1024 * 1024),
        name="solve_sensors",
    )(tau * pack_rows(fill(gram)), pack_rows(fill(target)), twice(fill(noise)), twice(prior))
    return solved[:, :share]


def shifted(shard, axis, by):
    size = lax.axis_size(axis)
    pairs = [(i, i + by) for i in range(size) if 0 <= i + by < size]
    return lax.ppermute(shard, axis, pairs)


def general_shards(
    y_obs,
    observed,
    day_factor,
    slot_factor,
    sensor_factor,
    prior_scale,
    neighbours,
    edge_weight,
    noise,
):
    rank = sensor_factor.shape[0]
    block_len = sensor_factor.shape[1]
    all_slots = lax.all_gather(slot_factor, "day", axis=0, tiled=True)
    features = (day_factor[:, None, :] * all_slots[None, :, :]).reshape(-1, rank)
    row_total = features.shape[0] * lax.axis_size("day")
    outer_rows = (features[:, :, None] * features[:, None, :]).reshape(-1, rank * rank)
    mask_half = observed.astype(jnp.bfloat16)
    weighted = mask_half * y_obs
    dims = (((0,), (0,)), ((), ()))
    gram_sums = lax.dot_general(outer_rows, mask_half, dims, preferred_element_type=jnp.float32)
    right_sums = lax.dot_general(features, weighted, dims, preferred_element_type=jnp.float32)
    pieces = []
    for offset in (2, 1, 0, -1, -2):
        if offset == 0:
            pieces.append(sensor_factor)
        else:
            pieces.append(shifted(sensor_factor, "sensor", offset))
    window = jnp.concatenate(pieces, axis=1)
    base_col = (lax.axis_index("sensor") - 2) * block_len
    columns = neighbours - base_col
    picked = jnp.take(window, columns, axis=1).astype(jnp.float32)
    pulled = jnp.einsum("rns,ns->rs", picked, edge_weight)
    prior_diag = 1.0 + jnp.sum(edge_weight, axis=0)
    tau = 4.0 / row_total
    sums = jnp.concatenate([gram_sums, right_sums], axis=0)
    sums = lax.psum_scatter(sums, "day", scatter_dimension=1, tiled=True)
    share_len = sums.shape[1]
    first_col = lax.axis_index("day") * share_len
    part = lambda array: lax.dynamic_slice_in_dim(array, first_col, share_len, array.ndim - 1)
    solved = solve_block(
        sums[: rank * rank].reshape(rank, rank, share_len),
        sums[rank * rank :],
        part(pulled),
        part(prior_diag),
        prior_scale,
        part(noise),
        tau,
    )
    return lax.all_gather(solved, "day", axis=1, tiled=True)


COUNTS = [4 - block // 2 for block in range(BLOCKS)]
STARTS = [64 * sum(COUNTS[:block]) for block in range(BLOCKS)]
PACKED_ROWS = 64 * sum(COUNTS)
OFFSETS = (-2, -1, 1, 2)
DAY_ROWS = 16


def pack_pair(even, odd, own):
    low = lane_low(even.shape)
    if own:
        return jnp.where(low, even, pltpu.roll(odd, HALF, 1))
    return jnp.where(low, pltpu.roll(even, HALF, 1), odd)


def split_pairs(rows):
    count = rows.shape[0] // 16
    pairs = rows.reshape(count, 2, 8, LANES)
    return pairs[:, 0].reshape(8 * count, LANES), pairs[:, 1].reshape(8 * count, LANES)


def sweep_kernel(
    tau,
    days,
    y_hbm,
    observed_hbm,
    day_hbm,
    slot_hbm,
    factor_hbm,
    scale_hbm,
    neighbour_hbm,
    weight_hbm,
    noise_hbm,
    out_ref,
    day_ref,
    slot_ref,
    factor_ref,
    scale_ref,
    neighbour_ref,
    weight_ref,
    noise_ref,
    y_ref,
    observed_ref,
    mask_ref,
    weighted_ref,
    sent_mask,
    got_mask,
    own_right,
    sent_right,
    got_right,
    slot_wide,
    sent_factors,
    got_factors,
    window,
    features,
    wide_features,
    half_features,
    gram,
    prior_ref,
    noise_own,
    packed_ref,
    peer_packed,
    found,
    cols,
    wide,
    inv_diag,
    halfway,
    load_sems,
    factor_sems,
    mask_sems,
    right_sems,
    window_send,
    window_recv,
    final_sems,
):
    day = lax.axis_index("day")
    sensor = lax.axis_index("sensor")
    sensors = lax.axis_size("sensor")
    rows = y_ref.shape[0]
    half_rows = rows // 2
    padded = mask_ref.shape[1]
    half_slots = slot_ref.shape[1]
    peer = {"day": 1 - day}
    mesh_id = pl.DeviceIdType.MESH
    f32, bf16 = jnp.float32, jnp.bfloat16

    barrier = pltpu.get_barrier_semaphore()
    pl.semaphore_signal(barrier, inc=1, device_id=peer, device_id_type=mesh_id)
    others = [lax.rem(sensor + sensors + offset, sensors) for offset in OFFSETS]
    for other in others:
        pl.semaphore_signal(barrier, inc=1, device_id={"sensor": other}, device_id_type=mesh_id)
    pairs = (
        (slot_hbm, slot_ref),
        (day_hbm, day_ref),
        (observed_hbm, observed_ref),
        (y_hbm, y_ref),
        (factor_hbm, factor_ref),
        (scale_hbm, scale_ref),
        (neighbour_hbm, neighbour_ref),
        (weight_hbm, weight_ref),
        (noise_hbm, noise_ref),
    )
    loads = []
    for index, (source, target) in enumerate(pairs):
        load = pltpu.make_async_copy(source, target, load_sems.at[index])
        load.start()
        loads.append(load)
    load_slots, load_days, load_mask, load_y, load_factor = loads[:5]

    def to_peer(source, target, sems):
        return pltpu.make_async_remote_copy(
            src_ref=source,
            dst_ref=target,
            send_sem=sems.at[0],
            recv_sem=sems.at[1],
            device_id=peer,
            device_id_type=mesh_id,
        )

    slot_wide[...] = jnp.zeros(slot_wide.shape, f32)
    load_slots.wait()
    slot_wide[pl.ds(0, RANK), pl.ds(0, half_slots)] = slot_ref[...].astype(f32)
    here = slot_wide[...].T[:half_slots]
    sent_factors[pl.ds(0, half_slots), :] = here.astype(bf16)
    load_days.wait()
    day_own = day_ref[...].astype(f32)
    day_own = jnp.concatenate([day_own, day_own], axis=1)
    tile_rows = lax.broadcasted_iota(jnp.int32, (DAY_ROWS, LANES), 0)
    day_tile = jnp.zeros((DAY_ROWS, LANES), f32)
    for index in range(days):
        day_tile = jnp.where(tile_rows == index, day_own[index : index + 1, :], day_tile)
    sent_factors[pl.ds(half_slots, DAY_ROWS), :] = day_tile.astype(bf16)

    def own_first(tile):
        return jnp.where(day == 0, tile, pltpu.roll(tile, HALF, 1))

    load_mask.wait()
    mask = own_first(observed_ref[...].astype(f32))
    mask_ref[0, pl.ds(0, rows), :] = mask.astype(bf16)
    sent_mask[...] = pack_pair(mask[:half_rows], mask[half_rows:], False).astype(bf16)

    load_factor.wait()
    pl.semaphore_wait(barrier, 1 + len(OFFSETS))
    factor_copy = to_peer(sent_factors, got_factors, factor_sems)
    factor_copy.start()
    mask_copy = to_peer(sent_mask, got_mask, mask_sems)
    mask_copy.start()
    window_copies = []
    for index, (offset, other) in enumerate(zip(OFFSETS, others)):
        copy = pltpu.make_async_remote_copy(
            src_ref=factor_ref,
            dst_ref=window.at[2 - offset],
            send_sem=window_send.at[index],
            recv_sem=window_recv.at[index],
            device_id={"sensor": other},
            device_id_type=mesh_id,
        )
        copy.start()
        window_copies.append(copy)

    load_y.wait()
    weighted = own_first(observed_ref[...].astype(f32) * y_ref[...].astype(f32))
    weighted_ref[pl.ds(0, rows), :] = weighted.astype(bf16)
    if padded > rows:
        empty = jnp.zeros((padded - rows, LANES), bf16)
        for part in range(2):
            mask_ref[part, pl.ds(rows, padded - rows), :] = empty
        weighted_ref[pl.ds(rows, padded - rows), :] = empty
        features[pl.ds(rows, padded - rows), :] = jnp.zeros((padded - rows, LANES), f32)

    factor_copy.wait()
    there = got_factors[pl.ds(0, half_slots), :].astype(f32)
    early = jnp.where(day == 0, here, there)
    late = jnp.where(day == 0, there, here)
    day_peer = got_factors[pl.ds(half_slots, DAY_ROWS), :].astype(f32)

    def make_features(part):
        day_rows = day_own if part == 0 else day_peer
        for index in range(days):
            row = day_rows[index : index + 1, :]
            at = index * 2 * half_slots
            features[pl.ds(at, half_slots), :] = early * row
            features[pl.ds(at + half_slots, half_slots), :] = late * row
        for index in range(padded // LANES):
            piece = features[pl.ds(index * LANES, LANES), :].T[:RANK]
            rounded = piece.astype(bf16)
            half_features[part, :, pl.ds(index * LANES, LANES)] = rounded
            wide_features[part, :, pl.ds(index * LANES, LANES)] = rounded.astype(f32)

    def gram_block(part, block):
        first = block // 2
        count = COUNTS[block]
        tiles = []
        for c in range(8):
            row = wide_features[part, pl.ds(8 * block + c, 1), :]
            row = jnp.broadcast_to(row, (16, padded)).astype(bf16)
            for q in range(first, 4):
                tiles.append(half_features[part, pl.ds(16 * q, 16), :] * row)
        rows_of_block = jnp.concatenate(tiles, axis=0)
        sums = jnp.dot(rows_of_block, mask_ref[part], preferred_element_type=f32)
        even, odd = split_pairs(sums)
        return pack_pair(even, odd, True)

    make_features(0)
    right = jnp.dot(half_features[0], weighted_ref[...], preferred_element_type=f32)
    even, odd = split_pairs(right)
    own_right[...] = pack_pair(even, odd, True)
    sent_right[...] = pack_pair(even, odd, False)
    right_copy = to_peer(sent_right, got_right, right_sems)
    right_copy.start()
    for block in range(BLOCKS):
        gram[pl.ds(STARTS[block], 64 * COUNTS[block]), :] = gram_block(0, block)
    make_features(1)

    for load in loads[5:]:
        load.wait()

    mine = (lax.broadcasted_iota(jnp.int32, (RANK, LANES), 1) >= HALF) == (day == 1)

    def spread_own(tile):
        return jnp.where(mine, tile, pltpu.roll(tile, HALF, 1))

    eye_rows = lax.broadcasted_iota(jnp.int32, (RANK, RANK), 0)
    eye_cols = lax.broadcasted_iota(jnp.int32, (RANK, RANK), 1)
    scale_row = jnp.broadcast_to(scale_ref[...], (RANK, RANK))
    scale = jnp.sum(jnp.where(eye_rows == eye_cols, scale_row, 0.0), axis=1, keepdims=True)
    scale = jnp.broadcast_to(scale, (RANK, LANES))
    prior_diag = 1.0 + jnp.sum(weight_ref[...], axis=0, keepdims=True)
    prior_ref[...] = scale * spread_own(jnp.broadcast_to(prior_diag, (RANK, LANES)))
    noise_own[...] = spread_own(noise_ref[...])

    base = (sensor - 2) * LANES
    column = neighbour_ref[...] - base
    weights = weight_ref[...]
    pulled = jnp.zeros((RANK, LANES), f32)
    for copy in window_copies:
        copy.wait()
    for slot in range(5):
        ids = lax.broadcasted_iota(jnp.int32, (LANES, LANES), 0) + slot * LANES
        picks = jnp.zeros((LANES, LANES), f32)
        for n in range(neighbour_ref.shape[0]):
            picks = picks + jnp.where(ids == column[n : n + 1, :], weights[n : n + 1, :], 0.0)
        high = picks.astype(bf16)
        low_part = (picks - high.astype(f32)).astype(bf16)
        source = factor_ref[...] if slot == 2 else window[slot]
        pulled = pulled + jnp.dot(source, high, preferred_element_type=f32)
        pulled = pulled + jnp.dot(source, low_part, preferred_element_type=f32)
    pulled = scale * spread_own(pulled)
    even, odd = split_pairs(pulled)
    pulled = jnp.where(lane_low(even.shape), even, odd)

    mask_copy.wait()
    mask_ref[1, pl.ds(0, half_rows), :] = got_mask[...]
    turned = pltpu.roll(got_mask[...].astype(f32), HALF, 1)
    mask_ref[1, pl.ds(half_rows, half_rows), :] = turned.astype(bf16)
    for block in range(BLOCKS):
        at = pl.ds(STARTS[block], 64 * COUNTS[block])
        gram[at, :] = tau * (gram[at, :] + gram_block(1, block))

    right_copy.wait()
    target = tau * (own_right[...] + got_right[...]) + pulled

    def load_columns(block):
        first = block // 2
        count = COUNTS[block]
        prior = prior_ref[pl.ds(8 * block, 8), :]
        columns = []
        for c in range(8):
            tiles = []
            for q in range(first, 4):
                tiles.append(gram[pl.ds(STARTS[block] + 8 * (c * count + q - first), 8), :])
            tiles[0] = tiles[0] + diagonal_tile(block, c, prior)
            columns.append(tiles)
        return columns

    packed = factor_and_solve(
        load_columns,
        [target[8 * q : 8 * q + 8, :] for q in range(4)],
        lambda block: noise_own[pl.ds(8 * block, 8), :],
        cols,
        wide,
        inv_diag,
        halfway,
        found,
    )
    for q in range(4):
        packed_ref[pl.ds(8 * q, 8), :] = packed[q]
    final_copy = to_peer(packed_ref, peer_packed, final_sems)
    final_copy.start()
    final_copy.wait()
    mine_tile = (lax.broadcasted_iota(jnp.int32, (8, LANES), 1) >= HALF) == (day == 1)
    for tile in range(8):
        theirs = both_halves(peer_packed[pl.ds(8 * (tile // 2), 8), :], tile % 2 == 1)
        at = pl.ds(8 * tile, 8)
        out_ref[at, :] = jnp.where(mine_tile, found[at, :], theirs)


def paired_shards(
    y_obs,
    observed,
    day_factor,
    slot_factor,
    sensor_factor,
    prior_scale,
    neighbours,
    edge_weight,
    noise,
):
    rows = y_obs.shape[0]
    padded = -(-rows // 256) * 256
    half_slots = slot_factor.shape[0]
    slot_lanes = -(-half_slots // LANES) * LANES
    days = day_factor.shape[0]
    tau = 4.0 / (2 * rows)
    vmem = pl.BlockSpec(memory_space=pltpu.VMEM)
    hbm = pl.BlockSpec(memory_space=pl.ANY)
    f32, bf16 = jnp.float32, jnp.bfloat16
    dma = pltpu.SemaphoreType.DMA
    return pl.pallas_call(
        functools.partial(sweep_kernel, tau, days),
        out_shape=pltpu.VMEM((RANK, LANES), f32),
        in_specs=[hbm] * 9,
        out_specs=vmem,
        scratch_shapes=[
            pltpu.VMEM(day_factor.shape, bf16),
            pltpu.VMEM((RANK, half_slots), bf16),
            pltpu.VMEM((RANK, LANES), bf16),
            pltpu.VMEM((1, RANK), f32),
            pltpu.VMEM(neighbours.shape, jnp.int32),
            pltpu.VMEM(edge_weight.shape, f32),
            pltpu.VMEM((RANK, LANES), f32),
            pltpu.VMEM((rows, LANES), bf16),
            pltpu.VMEM((rows, LANES), jnp.int32),
            pltpu.VMEM((2, padded, LANES), bf16),
            pltpu.VMEM((padded, LANES), bf16),
            pltpu.VMEM((rows // 2, LANES), bf16),
            pltpu.VMEM((rows // 2, LANES), bf16),
            pltpu.VMEM((32, LANES), f32),
            pltpu.VMEM((32, LANES), f32),
            pltpu.VMEM((32, LANES), f32),
            pltpu.VMEM((LANES, slot_lanes), f32),
            pltpu.VMEM((half_slots + DAY_ROWS, LANES), bf16),
            pltpu.VMEM((half_slots + DAY_ROWS, LANES), bf16),
            pltpu.VMEM((5, RANK, LANES), bf16),
            pltpu.VMEM((padded, LANES), f32),
            pltpu.VMEM((2, RANK, padded), f32),
            pltpu.VMEM((2, RANK, padded), bf16),
            pltpu.VMEM((PACKED_ROWS, LANES), f32),
            pltpu.VMEM((RANK, LANES), f32),
            pltpu.VMEM((RANK, LANES), f32),
            pltpu.VMEM((32, LANES), f32),
            pltpu.VMEM((32, LANES), f32),
            pltpu.VMEM((RANK, LANES), f32),
        ]
        + solver_scratch()
        + [dma((9,)), dma((2,)), dma((2,)), dma((2,)), dma((4,)), dma((4,)), dma((2,))],
        compiler_params=pltpu.CompilerParams(
            collective_id=0, has_side_effects=True, vmem_limit_bytes=VMEM_BYTES
        ),
        name="sweep_sensors",
    )(
        y_obs,
        observed,
        day_factor,
        slot_factor.T,
        sensor_factor,
        prior_scale.reshape(1, RANK),
        neighbours,
        edge_weight,
        noise,
    )


def solution(mesh):
    sizes = dict(mesh.shape)

    def shards(*arrays):
        y_obs, slot_factor = arrays[0], arrays[3]
        fits = sizes["day"] == 2 and sizes["sensor"] >= 5 and y_obs.shape[1] == LANES
        fits = fits and y_obs.shape[0] % 32 == 0 and slot_factor.shape[0] % 16 == 0
        fits = fits and arrays[2].shape[0] <= DAY_ROWS
        return paired_shards(*arrays) if fits else general_shards(*arrays)

    return jax.shard_map(
        shards,
        mesh=mesh,
        in_specs=(
            P("day", "sensor"),
            P("day", "sensor"),
            P("day", None),
            P("day", None),
            P(None, "sensor"),
            P(),
            P(None, "sensor"),
            P(None, "sensor"),
            P(None, "sensor"),
        ),
        out_specs=P(None, "sensor"),
        check_vma=False,
    )
```

```python
import functools

import jax
import jax.numpy as jnp
from jax import lax
from jax.experimental import pallas as pl
from jax.experimental.pallas import tpu as pltpu
from jax.sharding import PartitionSpec as P

RANK = 64
LANES = 128
HALF = 64
BLOCKS = RANK // 8
VMEM_BYTES = 60 * 1024 * 1024


def lane_low(shape):
    return lax.broadcasted_iota(jnp.int32, shape, len(shape) - 1) < HALF


def both_halves(tile, upper):
    other = pltpu.roll(tile, HALF, 1)
    low = lane_low(tile.shape)
    return jnp.where(low, other, tile) if upper else jnp.where(low, tile, other)


def row_of(tile, index):
    return jnp.broadcast_to(tile[index : index + 1, :], tile.shape)


def factor_and_solve(load_columns, target, noise_tile, cols, wide, inv_diag, halfway, found):
    target = list(target)
    for block in range(BLOCKS):
        first = block // 2
        upper = block % 2 == 1
        count = 4 - first
        columns = load_columns(block)
        if block > 0:

            def subtract(k, carry):
                done = [cols[k, pl.ds(8 * q, 8), :] for q in range(first, 4)]
                out = []
                for c in range(8):
                    scale = jnp.broadcast_to(wide[k, pl.ds(8 * block + c, 1), :], (8, LANES))
                    out.extend(carry[c * count + q] - done[q] * scale for q in range(count))
                return tuple(out)

            flat = tuple(tile for column in columns for tile in column)
            flat = lax.fori_loop(0, 8 * block, subtract, flat, unroll=4)
            columns = [list(flat[c * count : (c + 1) * count]) for c in range(8)]
        corner = [both_halves(column[0], upper) for column in columns]
        side = both_halves(target[first], upper)
        for c in range(8):
            j = 8 * block + c
            inverse = lax.rsqrt(row_of(corner[c], c))
            corner[c] = corner[c] * inverse
            columns[c] = [tile * inverse for tile in columns[c]]
            solved = row_of(side, c) * inverse
            side = side - corner[c] * solved
            for q in range(count):
                target[first + q] = target[first + q] - columns[c][q] * solved
            for later in range(c + 1, 8):
                scale = row_of(corner[c], later)
                corner[later] = corner[later] - corner[c] * scale
                columns[later] = [
                    tile - own * scale for tile, own in zip(columns[later], columns[c])
                ]
            inv_diag[j] = inverse
            halfway[pl.ds(j, 1), :] = solved[0:1, :]
        for c in range(8):
            j = 8 * block + c
            for q in range(count):
                tile = columns[c][q]
                row = 16 * (first + q)
                cols[j, pl.ds(8 * (first + q), 8), :] = tile
                if row >= 8 * block:
                    wide[j, pl.ds(row, 8), :] = both_halves(tile, False)
                wide[j, pl.ds(row + 8, 8), :] = both_halves(tile, True)

    packed = [None] * 4
    low = lane_low((8, LANES))
    below = None
    for block in reversed(range(BLOCKS)):
        first = block // 2
        upper = block % 2 == 1
        right = halfway[pl.ds(8 * block, 8), :] + noise_tile(block)
        remain = []
        for c in range(8):
            j = 8 * block + c
            total = row_of(right, c)
            parts = None
            for q in range(first, 4):
                if q == first and upper:
                    continue
                if q == first:
                    term = jnp.where(low, 0.0, cols[j, pl.ds(8 * q, 8), :] * below)
                else:
                    term = cols[j, pl.ds(8 * q, 8), :] * packed[q]
                parts = term if parts is None else parts + term
            if parts is not None:
                sums = jnp.sum(parts, axis=0, keepdims=True)
                sums = jnp.broadcast_to(sums, (8, LANES))
                total = total - (sums + pltpu.roll(sums, HALF, 1))
            remain.append(total)
        values = [None] * 8
        for c in reversed(range(8)):
            values[c] = remain[c] * inv_diag[8 * block + c]
            for earlier in range(c):
                scale = jnp.broadcast_to(
                    wide[8 * block + earlier, pl.ds(8 * block + c, 1), :], (8, LANES)
                )
                remain[earlier] = remain[earlier] - scale * values[c]
        rows = lax.broadcasted_iota(jnp.int32, (8, LANES), 0)
        tile = values[0]
        for c in range(1, 8):
            tile = jnp.where(rows == c, values[c], tile)
        found[pl.ds(8 * block, 8), :] = tile
        if upper:
            below = tile
        else:
            packed[first] = jnp.where(low, tile, below)
            below = None
    return packed


def diagonal_tile(block, c, value):
    shape = (8, LANES)
    rows = lax.broadcasted_iota(jnp.int32, shape, 0)
    low = lane_low(shape)
    half = low if block % 2 == 0 else jnp.logical_not(low)
    return jnp.where((rows == c) & half, value, 0.0)


def solve_kernel(squares, target, noise, prior, out, cols, wide, inv_diag, halfway):
    def load_columns(block):
        first = block // 2
        own = prior[pl.ds(8 * block, 8), :]
        columns = []
        for c in range(8):
            j = 8 * block + c
            tiles = [squares[j, pl.ds(8 * q, 8), :] for q in range(first, 4)]
            tiles[0] = tiles[0] + diagonal_tile(block, c, own)
            columns.append(tiles)
        return columns

    targets = [target[pl.ds(8 * q, 8), :] for q in range(4)]
    factor_and_solve(
        load_columns,
        targets,
        lambda block: noise[pl.ds(8 * block, 8), :],
        cols,
        wide,
        inv_diag,
        halfway,
        out,
    )


def solver_scratch():
    return [
        pltpu.VMEM((RANK, 32, LANES), jnp.float32),
        pltpu.VMEM((RANK, RANK, LANES), jnp.float32),
        pltpu.VMEM((RANK, 8, LANES), jnp.float32),
        pltpu.VMEM((RANK, LANES), jnp.float32),
    ]


def pack_rows(rows):
    lead = rows.shape[:-2]
    split = rows.reshape(lead + (4, 2, 8, HALF))
    return jnp.swapaxes(split, -3, -2).reshape(lead + (32, LANES))


def solve_block(gram, right, pulled, prior_diag, prior_scale, noise, tau):
    share = right.shape[1]

    def fill(array, value=0.0):
        pad = [(0, 0)] * (array.ndim - 1) + [(0, HALF - share)]
        return jnp.pad(array, pad, constant_values=value)

    target = tau * right + prior_scale[:, None] * pulled
    prior = prior_scale[:, None] * fill(prior_diag, 1.0)[None, :]
    twice = lambda array: jnp.concatenate([array, array], axis=1)
    spec = pl.BlockSpec(memory_space=pltpu.VMEM)
    solved = pl.pallas_call(
        solve_kernel,
        out_shape=jax.ShapeDtypeStruct((RANK, LANES), jnp.float32),
        in_specs=[spec] * 4,
        out_specs=spec,
        scratch_shapes=solver_scratch(),
        compiler_params=pltpu.CompilerParams(vmem_limit_bytes=24 * 1024 * 1024),
        name="solve_sensors",
    )(tau * pack_rows(fill(gram)), pack_rows(fill(target)), twice(fill(noise)), twice(prior))
    return solved[:, :share]


def shifted(shard, axis, by):
    size = lax.axis_size(axis)
    pairs = [(i, i + by) for i in range(size) if 0 <= i + by < size]
    return lax.ppermute(shard, axis, pairs)


def general_shards(
    y_obs,
    observed,
    day_factor,
    slot_factor,
    sensor_factor,
    prior_scale,
    neighbours,
    edge_weight,
    noise,
):
    rank = sensor_factor.shape[0]
    block_len = sensor_factor.shape[1]
    all_slots = lax.all_gather(slot_factor, "day", axis=0, tiled=True)
    features = (day_factor[:, None, :] * all_slots[None, :, :]).reshape(-1, rank)
    row_total = features.shape[0] * lax.axis_size("day")
    outer_rows = (features[:, :, None] * features[:, None, :]).reshape(-1, rank * rank)
    mask_half = observed.astype(jnp.bfloat16)
    weighted = mask_half * y_obs
    dims = (((0,), (0,)), ((), ()))
    gram_sums = lax.dot_general(outer_rows, mask_half, dims, preferred_element_type=jnp.float32)
    right_sums = lax.dot_general(features, weighted, dims, preferred_element_type=jnp.float32)
    pieces = []
    for offset in (2, 1, 0, -1, -2):
        if offset == 0:
            pieces.append(sensor_factor)
        else:
            pieces.append(shifted(sensor_factor, "sensor", offset))
    window = jnp.concatenate(pieces, axis=1)
    base_col = (lax.axis_index("sensor") - 2) * block_len
    columns = neighbours - base_col
    picked = jnp.take(window, columns, axis=1).astype(jnp.float32)
    pulled = jnp.einsum("rns,ns->rs", picked, edge_weight)
    prior_diag = 1.0 + jnp.sum(edge_weight, axis=0)
    tau = 4.0 / row_total
    sums = jnp.concatenate([gram_sums, right_sums], axis=0)
    sums = lax.psum_scatter(sums, "day", scatter_dimension=1, tiled=True)
    share_len = sums.shape[1]
    first_col = lax.axis_index("day") * share_len
    part = lambda array: lax.dynamic_slice_in_dim(array, first_col, share_len, array.ndim - 1)
    solved = solve_block(
        sums[: rank * rank].reshape(rank, rank, share_len),
        sums[rank * rank :],
        part(pulled),
        part(prior_diag),
        prior_scale,
        part(noise),
        tau,
    )
    return lax.all_gather(solved, "day", axis=1, tiled=True)


COUNTS = [4 - block // 2 for block in range(BLOCKS)]
STARTS = [64 * sum(COUNTS[:block]) for block in range(BLOCKS)]
PACKED_ROWS = 64 * sum(COUNTS)
OFFSETS = (-2, -1, 1, 2)
DAY_ROWS = 16


def pack_pair(even, odd, own):
    low = lane_low(even.shape)
    if own:
        return jnp.where(low, even, pltpu.roll(odd, HALF, 1))
    return jnp.where(low, pltpu.roll(even, HALF, 1), odd)


def split_pairs(rows):
    count = rows.shape[0] // 16
    pairs = rows.reshape(count, 2, 8, LANES)
    return pairs[:, 0].reshape(8 * count, LANES), pairs[:, 1].reshape(8 * count, LANES)


def sweep_kernel(
    tau,
    days,
    y_hbm,
    observed_hbm,
    day_hbm,
    slot_hbm,
    factor_hbm,
    scale_hbm,
    neighbour_hbm,
    weight_hbm,
    noise_hbm,
    out_ref,
    day_ref,
    slot_ref,
    factor_ref,
    scale_ref,
    neighbour_ref,
    weight_ref,
    noise_ref,
    y_ref,
    observed_ref,
    mask_ref,
    weighted_ref,
    sent_mask,
    got_mask,
    own_right,
    sent_right,
    got_right,
    slot_wide,
    sent_factors,
    got_factors,
    window,
    features,
    wide_features,
    half_features,
    gram,
    prior_ref,
    noise_own,
    packed_ref,
    peer_packed,
    found,
    cols,
    wide,
    inv_diag,
    halfway,
    load_sems,
    factor_sems,
    mask_sems,
    right_sems,
    window_send,
    window_recv,
    final_sems,
):
    day = lax.axis_index("day")
    sensor = lax.axis_index("sensor")
    sensors = lax.axis_size("sensor")
    rows = y_ref.shape[0]
    half_rows = rows // 2
    padded = mask_ref.shape[1]
    half_slots = slot_ref.shape[1]
    peer = {"day": 1 - day}
    mesh_id = pl.DeviceIdType.MESH
    f32, bf16 = jnp.float32, jnp.bfloat16

    barrier = pltpu.get_barrier_semaphore()
    pl.semaphore_signal(barrier, inc=1, device_id=peer, device_id_type=mesh_id)
    others = [lax.rem(sensor + sensors + offset, sensors) for offset in OFFSETS]
    for other in others:
        pl.semaphore_signal(barrier, inc=1, device_id={"sensor": other}, device_id_type=mesh_id)
    pairs = (
        (slot_hbm, slot_ref),
        (day_hbm, day_ref),
        (observed_hbm, observed_ref),
        (y_hbm, y_ref),
        (factor_hbm, factor_ref),
        (scale_hbm, scale_ref),
        (neighbour_hbm, neighbour_ref),
        (weight_hbm, weight_ref),
        (noise_hbm, noise_ref),
    )
    loads = []
    for index, (source, target) in enumerate(pairs):
        load = pltpu.make_async_copy(source, target, load_sems.at[index])
        load.start()
        loads.append(load)
    load_slots, load_days, load_mask, load_y, load_factor = loads[:5]

    def to_peer(source, target, sems):
        return pltpu.make_async_remote_copy(
            src_ref=source,
            dst_ref=target,
            send_sem=sems.at[0],
            recv_sem=sems.at[1],
            device_id=peer,
            device_id_type=mesh_id,
        )

    slot_wide[...] = jnp.zeros(slot_wide.shape, f32)
    load_slots.wait()
    slot_wide[pl.ds(0, RANK), pl.ds(0, half_slots)] = slot_ref[...].astype(f32)
    here = slot_wide[...].T[:half_slots]
    sent_factors[pl.ds(0, half_slots), :] = here.astype(bf16)
    load_days.wait()
    day_own = day_ref[...].astype(f32)
    day_own = jnp.concatenate([day_own, day_own], axis=1)
    tile_rows = lax.broadcasted_iota(jnp.int32, (DAY_ROWS, LANES), 0)
    day_tile = jnp.zeros((DAY_ROWS, LANES), f32)
    for index in range(days):
        day_tile = jnp.where(tile_rows == index, day_own[index : index + 1, :], day_tile)
    sent_factors[pl.ds(half_slots, DAY_ROWS), :] = day_tile.astype(bf16)

    def own_first(tile):
        return jnp.where(day == 0, tile, pltpu.roll(tile, HALF, 1))

    load_mask.wait()
    mask = own_first(observed_ref[...].astype(f32))
    mask_ref[0, pl.ds(0, rows), :] = mask.astype(bf16)
    sent_mask[...] = pack_pair(mask[:half_rows], mask[half_rows:], False).astype(bf16)

    load_factor.wait()
    pl.semaphore_wait(barrier, 1 + len(OFFSETS))
    factor_copy = to_peer(sent_factors, got_factors, factor_sems)
    factor_copy.start()
    mask_copy = to_peer(sent_mask, got_mask, mask_sems)
    mask_copy.start()
    window_copies = []
    for index, (offset, other) in enumerate(zip(OFFSETS, others)):
        copy = pltpu.make_async_remote_copy(
            src_ref=factor_ref,
            dst_ref=window.at[2 - offset],
            send_sem=window_send.at[index],
            recv_sem=window_recv.at[index],
            device_id={"sensor": other},
            device_id_type=mesh_id,
        )
        copy.start()
        window_copies.append(copy)

    load_y.wait()
    weighted = own_first(observed_ref[...].astype(f32) * y_ref[...].astype(f32))
    weighted_ref[pl.ds(0, rows), :] = weighted.astype(bf16)
    if padded > rows:
        empty = jnp.zeros((padded - rows, LANES), bf16)
        for part in range(2):
            mask_ref[part, pl.ds(rows, padded - rows), :] = empty
        weighted_ref[pl.ds(rows, padded - rows), :] = empty
        features[pl.ds(rows, padded - rows), :] = jnp.zeros((padded - rows, LANES), f32)

    factor_copy.wait()
    there = got_factors[pl.ds(0, half_slots), :].astype(f32)
    early = jnp.where(day == 0, here, there)
    late = jnp.where(day == 0, there, here)
    day_peer = got_factors[pl.ds(half_slots, DAY_ROWS), :].astype(f32)

    def make_features(part):
        day_rows = day_own if part == 0 else day_peer
        for index in range(days):
            row = day_rows[index : index + 1, :]
            at = index * 2 * half_slots
            features[pl.ds(at, half_slots), :] = early * row
            features[pl.ds(at + half_slots, half_slots), :] = late * row
        for index in range(padded // LANES):
            piece = features[pl.ds(index * LANES, LANES), :].T[:RANK]
            rounded = piece.astype(bf16)
            half_features[part, :, pl.ds(index * LANES, LANES)] = rounded
            wide_features[part, :, pl.ds(index * LANES, LANES)] = rounded.astype(f32)

    def gram_block(part, block):
        first = block // 2
        count = COUNTS[block]
        tiles = []
        for c in range(8):
            row = wide_features[part, pl.ds(8 * block + c, 1), :]
            row = jnp.broadcast_to(row, (16, padded)).astype(bf16)
            for q in range(first, 4):
                tiles.append(half_features[part, pl.ds(16 * q, 16), :] * row)
        rows_of_block = jnp.concatenate(tiles, axis=0)
        sums = jnp.dot(rows_of_block, mask_ref[part], preferred_element_type=f32)
        even, odd = split_pairs(sums)
        return pack_pair(even, odd, True)

    make_features(0)
    right = jnp.dot(half_features[0], weighted_ref[...], preferred_element_type=f32)
    even, odd = split_pairs(right)
    own_right[...] = pack_pair(even, odd, True)
    sent_right[...] = pack_pair(even, odd, False)
    right_copy = to_peer(sent_right, got_right, right_sems)
    right_copy.start()
    for block in range(BLOCKS):
        gram[pl.ds(STARTS[block], 64 * COUNTS[block]), :] = gram_block(0, block)
    make_features(1)

    for load in loads[5:]:
        load.wait()

    mine = (lax.broadcasted_iota(jnp.int32, (RANK, LANES), 1) >= HALF) == (day == 1)

    def spread_own(tile):
        return jnp.where(mine, tile, pltpu.roll(tile, HALF, 1))

    eye_rows = lax.broadcasted_iota(jnp.int32, (RANK, RANK), 0)
    eye_cols = lax.broadcasted_iota(jnp.int32, (RANK, RANK), 1)
    scale_row = jnp.broadcast_to(scale_ref[...], (RANK, RANK))
    scale = jnp.sum(jnp.where(eye_rows == eye_cols, scale_row, 0.0), axis=1, keepdims=True)
    scale = jnp.broadcast_to(scale, (RANK, LANES))
    prior_diag = 1.0 + jnp.sum(weight_ref[...], axis=0, keepdims=True)
    prior_ref[...] = scale * spread_own(jnp.broadcast_to(prior_diag, (RANK, LANES)))
    noise_own[...] = spread_own(noise_ref[...])

    base = (sensor - 2) * LANES
    column = neighbour_ref[...] - base
    weights = weight_ref[...]
    pulled = jnp.zeros((RANK, LANES), f32)
    for copy in window_copies:
        copy.wait()
    for slot in range(5):
        ids = lax.broadcasted_iota(jnp.int32, (LANES, LANES), 0) + slot * LANES
        picks = jnp.zeros((LANES, LANES), f32)
        for n in range(neighbour_ref.shape[0]):
            picks = picks + jnp.where(ids == column[n : n + 1, :], weights[n : n + 1, :], 0.0)
        high = picks.astype(bf16)
        low_part = (picks - high.astype(f32)).astype(bf16)
        source = factor_ref[...] if slot == 2 else window[slot]
        pulled = pulled + jnp.dot(source, high, preferred_element_type=f32)
        pulled = pulled + jnp.dot(source, low_part, preferred_element_type=f32)
    pulled = scale * spread_own(pulled)
    even, odd = split_pairs(pulled)
    pulled = jnp.where(lane_low(even.shape), even, odd)

    mask_copy.wait()
    mask_ref[1, pl.ds(0, half_rows), :] = got_mask[...]
    turned = pltpu.roll(got_mask[...].astype(f32), HALF, 1)
    mask_ref[1, pl.ds(half_rows, half_rows), :] = turned.astype(bf16)
    for block in range(BLOCKS):
        at = pl.ds(STARTS[block], 64 * COUNTS[block])
        gram[at, :] = tau * (gram[at, :] + gram_block(1, block))

    right_copy.wait()
    target = tau * (own_right[...] + got_right[...]) + pulled

    def load_columns(block):
        first = block // 2
        count = COUNTS[block]
        prior = prior_ref[pl.ds(8 * block, 8), :]
        columns = []
        for c in range(8):
            tiles = []
            for q in range(first, 4):
                tiles.append(gram[pl.ds(STARTS[block] + 8 * (c * count + q - first), 8), :])
            tiles[0] = tiles[0] + diagonal_tile(block, c, prior)
            columns.append(tiles)
        return columns

    packed = factor_and_solve(
        load_columns,
        [target[8 * q : 8 * q + 8, :] for q in range(4)],
        lambda block: noise_own[pl.ds(8 * block, 8), :],
        cols,
        wide,
        inv_diag,
        halfway,
        found,
    )
    for q in range(4):
        packed_ref[pl.ds(8 * q, 8), :] = packed[q]
    final_copy = to_peer(packed_ref, peer_packed, final_sems)
    final_copy.start()
    final_copy.wait()
    mine_tile = (lax.broadcasted_iota(jnp.int32, (8, LANES), 1) >= HALF) == (day == 1)
    for tile in range(8):
        theirs = both_halves(peer_packed[pl.ds(8 * (tile // 2), 8), :], tile % 2 == 1)
        at = pl.ds(8 * tile, 8)
        out_ref[at, :] = jnp.where(mine_tile, found[at, :], theirs)


def paired_shards(
    y_obs,
    observed,
    day_factor,
    slot_factor,
    sensor_factor,
    prior_scale,
    neighbours,
    edge_weight,
    noise,
):
    rows = y_obs.shape[0]
    padded = -(-rows // 256) * 256
    half_slots = slot_factor.shape[0]
    slot_lanes = -(-half_slots // LANES) * LANES
    days = day_factor.shape[0]
    tau = 4.0 / (2 * rows)
    vmem = pl.BlockSpec(memory_space=pltpu.VMEM)
    hbm = pl.BlockSpec(memory_space=pl.ANY)
    f32, bf16 = jnp.float32, jnp.bfloat16
    dma = pltpu.SemaphoreType.DMA
    return pl.pallas_call(
        functools.partial(sweep_kernel, tau, days),
        out_shape=pltpu.VMEM((RANK, LANES), f32),
        in_specs=[hbm] * 9,
        out_specs=vmem,
        scratch_shapes=[
            pltpu.VMEM(day_factor.shape, bf16),
            pltpu.VMEM((RANK, half_slots), bf16),
            pltpu.VMEM((RANK, LANES), bf16),
            pltpu.VMEM((1, RANK), f32),
            pltpu.VMEM(neighbours.shape, jnp.int32),
            pltpu.VMEM(edge_weight.shape, f32),
            pltpu.VMEM((RANK, LANES), f32),
            pltpu.VMEM((rows, LANES), bf16),
            pltpu.VMEM((rows, LANES), jnp.int32),
            pltpu.VMEM((2, padded, LANES), bf16),
            pltpu.VMEM((padded, LANES), bf16),
            pltpu.VMEM((rows // 2, LANES), bf16),
            pltpu.VMEM((rows // 2, LANES), bf16),
            pltpu.VMEM((32, LANES), f32),
            pltpu.VMEM((32, LANES), f32),
            pltpu.VMEM((32, LANES), f32),
            pltpu.VMEM((LANES, slot_lanes), f32),
            pltpu.VMEM((half_slots + DAY_ROWS, LANES), bf16),
            pltpu.VMEM((half_slots + DAY_ROWS, LANES), bf16),
            pltpu.VMEM((5, RANK, LANES), bf16),
            pltpu.VMEM((padded, LANES), f32),
            pltpu.VMEM((2, RANK, padded), f32),
            pltpu.VMEM((2, RANK, padded), bf16),
            pltpu.VMEM((PACKED_ROWS, LANES), f32),
            pltpu.VMEM((RANK, LANES), f32),
            pltpu.VMEM((RANK, LANES), f32),
            pltpu.VMEM((32, LANES), f32),
            pltpu.VMEM((32, LANES), f32),
            pltpu.VMEM((RANK, LANES), f32),
        ]
        + solver_scratch()
        + [dma((9,)), dma((2,)), dma((2,)), dma((2,)), dma((4,)), dma((4,)), dma((2,))],
        compiler_params=pltpu.CompilerParams(
            collective_id=0, has_side_effects=True, vmem_limit_bytes=VMEM_BYTES
        ),
        name="sweep_sensors",
    )(
        y_obs,
        observed,
        day_factor,
        slot_factor.T,
        sensor_factor,
        prior_scale.reshape(1, RANK),
        neighbours,
        edge_weight,
        noise,
    )


def solution(mesh):
    sizes = dict(mesh.shape)

    def shards(*arrays):
        y_obs, slot_factor = arrays[0], arrays[3]
        fits = sizes["day"] == 2 and sizes["sensor"] >= 5 and y_obs.shape[1] == LANES
        fits = fits and y_obs.shape[0] % 32 == 0 and slot_factor.shape[0] % 16 == 0
        fits = fits and arrays[2].shape[0] <= DAY_ROWS
        return paired_shards(*arrays) if fits else general_shards(*arrays)

    return jax.shard_map(
        shards,
        mesh=mesh,
        in_specs=(
            P("day", "sensor"),
            P("day", "sensor"),
            P("day", None),
            P("day", None),
            P(None, "sensor"),
            P(),
            P(None, "sensor"),
            P(None, "sensor"),
            P(None, "sensor"),
        ),
        out_specs=P(None, "sensor"),
        check_vma=False,
    )
```
